256 devices in a mesh: sample: 2 (over z_hi), space: 8 (over y, core), filt: 16 (over z_lo, x).
Axes of the slice: x: 4, y: 4, z: 8 (z_hi: 2, z_lo: 4; z = z_hi * 4 + z_lo), core: 2. Of those that a mesh axis runs over, the one named last changes fastest.
Arguments:
- act_in: bfloat16 [2, 64, 16, 16, 128], P('sample', None, 'space'), may hold values from -6 to 6
- w_first: bfloat16 [27, 64, 128], P(None, None, 'filt'), may hold values from -0.15625 to 0.15625
- w_second: bfloat16 [27, 128, 128], P(None, None, 'filt'), may hold values from -0.109375 to 0.109375
- grad_out: bfloat16 [2, 128, 16, 16, 128], P('sample', 'filt', 'space'), may hold values from -6 to 6
Outputs:
- y_out: bfloat16 [2, 128, 16, 16, 128], P('sample', 'filt', 'space')
- grad_w_first: float32 [27, 64, 128], P(None, None, 'filt')
- grad_w_second: float32 [27, 128, 128], P(None, None, 'filt')
The draws below stay inside these ranges and needn't reach their ends.
All inputs are finite; a program needn't handle non-finite values.
Results may differ from the reference program's by a relative error of at most 0.0054.
Values may be sent and summed in bfloat16 or wider, within the bound.
No kernel may reach another device: no remote copies, remote signals or barrier semaphores. Data moves between devices by JAX's collectives and lax.ppermute only.
A program may use at most 64 MiB of HBM per device.

```python
import math
import jax
import jax.numpy as jnp
from jax import lax

CIN = 64
COUT = 128
WID = 128
SAMPLES = 2
DEPTH = 16
HGT = 16


def level_of(rng, dims, cuts, least, top_value):
    loudness = 1.0
    for dim, parts in cuts:
        heights = jax.random.uniform(jax.random.fold_in(jax.random.fold_in(rng, 6), dim), (parts,), jnp.float32, least / len(cuts), top_value / len(cuts))
        loudness = loudness * jnp.repeat(jnp.exp(heights), dims[dim] // parts).reshape((-1,) + (1,) * (len(dims) - 1 - dim))
    return loudness


def gaussian(rng, dims, scale, limit, pieces=(), held_as=jnp.bfloat16):
    drawn = scale * jax.random.normal(rng, dims, jnp.float32)
    if pieces:
        drawn = drawn * level_of(rng, dims, pieces, -0.22, 0.18)
    return jnp.clip(drawn, -limit, limit).astype(held_as)


def setup_inputs(seed: int = 0) -> dict:
    splits = jax.random.split(jax.random.key(seed), 5)
    act_in = gaussian(splits[0], (SAMPLES, CIN, DEPTH, HGT, WID), 1.0, 6.0, ((0, 2), (2, 8)))
    w_first = gaussian(splits[1], (27, CIN, COUT), (27 * CIN) ** -0.5, 0.15625, ((2, 16),))
    w_second = gaussian(splits[2], (27, COUT, COUT), (27 * COUT) ** -0.5, 0.109375, ((2, 16),))
    grad_out = gaussian(splits[3], (SAMPLES, COUT, DEPTH, HGT, WID), 1.0, 6.0, ((0, 2), (1, 16), (2, 8)))
    return dict(act_in=act_in, w_first=w_first, w_second=w_second, grad_out=grad_out)


def correlate(source, kernel, rim_pad):
    taps = kernel.reshape(3, 3, 3, kernel.shape[1], kernel.shape[2])
    return lax.conv_general_dilated(source[None], taps, (1, 1, 1), ((0, 0), (rim_pad, rim_pad), (1, 1)), dimension_numbers=('NCDHW', 'DHWIO', 'NCDHW'), preferred_element_type=jnp.float32)[0]

def transpose_correlate(gradient, kernel, rim_pad):
    taps = kernel.reshape(3, 3, 3, kernel.shape[1], kernel.shape[2])[::-1, ::-1, ::-1]
    return lax.conv_general_dilated(gradient[None], taps, (1, 1, 1), ((0, 0), (rim_pad, rim_pad), (1, 1)), dimension_numbers=('NCDHW', 'DHWOI', 'NCDHW'), preferred_element_type=jnp.float32)[0]

def kernel_gradient(source, gradient, rim_pad):
    result = lax.conv_general_dilated(source[None], gradient[None], (1, 1, 1), ((0, 0), (rim_pad, rim_pad), (1, 1)), dimension_numbers=('CNDHW', 'IODHW', 'NCDHW'), preferred_element_type=jnp.float32)
    return jnp.transpose(result, (2, 3, 4, 0, 1)).reshape(27, source.shape[0], gradient.shape[0])

def silu_slope(value):
    logistic = jax.nn.sigmoid(value)
    return logistic * (1.0 + value * (1.0 - logistic))

def reference(act_in, w_first, w_second, grad_out):
    depth_pad = ((0, 0), (1, 1), (0, 0), (0, 0))
    outputs = []
    total_first = jnp.zeros(w_first.shape, jnp.float32)
    total_second = jnp.zeros(w_second.shape, jnp.float32)
    for which in range(SAMPLES):
        padded_in = jnp.pad(act_in[which], depth_pad)
        z_first = correlate(padded_in, w_first, 1)
        act = jax.nn.silu(z_first).astype(jnp.bfloat16)
        padded_act = jnp.pad(act, depth_pad)
        z_second = correlate(padded_act, w_second, 1)
        outputs.append(jax.nn.silu(z_second).astype(jnp.bfloat16))
        grad_second = (grad_out[which].astype(jnp.float32) * silu_slope(z_second)).astype(jnp.bfloat16)
        padded_grad = jnp.pad(grad_second, depth_pad)
        back_first = transpose_correlate(padded_grad, w_second, 1)
        grad_first = (back_first * silu_slope(z_first)).astype(jnp.bfloat16)
        total_second = total_second + kernel_gradient(padded_act, grad_second, 1)
        total_first = total_first + kernel_gradient(padded_in, grad_first, 1)
    factor = 1.0 / math.sqrt(SAMPLES * DEPTH * HGT * WID)
    return (jnp.stack(outputs), total_first * factor, total_second * factor)
```

```python
import jax
import jax.numpy as jnp
from jax import lax
from jax.experimental import pallas as pl
from jax.experimental.pallas import tpu as pltpu
from jax.sharding import PartitionSpec as P

F32 = jnp.float32
BF16 = jnp.bfloat16
W = 128
K1, K2 = 27 * 64, 27 * 128
K1P = 1792
KB = 896
VMEM = pl.BlockSpec(memory_space=pltpu.VMEM)
NT = (((1,), (1,)), ((), ()))


def run(kernel, outs, args, scratch=()):
    return pl.pallas_call(
        kernel,
        out_shape=outs,
        in_specs=[VMEM] * len(args),
        out_specs=[VMEM] * len(outs),
        scratch_shapes=list(scratch),
        compiler_params=pltpu.CompilerParams(vmem_limit_bytes=48 * 1024 * 1024),
    )(*args)


def sds(shape, dtype):
    return jax.ShapeDtypeStruct(shape, dtype)


def split():
    f = lax.axis_index("filt")
    return lax.rem(f, 4), lax.div(f, 4)


def xor(a, k):
    return lax.bitwise_xor(a, jnp.int32(k))


def rows8(i):
    return pl.ds(pl.multiple_of(i * 8, 8), 8)


def rows32(i):
    return pl.ds(pl.multiple_of(i * 32, 32), 32)


def shifted(x):
    lane = lax.broadcasted_iota(jnp.int32, x.shape, 1)
    left = jnp.where(lane == 0, 0.0, pltpu.roll(x, 1, 1))
    right = jnp.where(lane == W - 1, 0.0, pltpu.roll(x, W - 1, 1))
    return left, x, right


def logistic(v):
    return 1.0 / (1.0 + jnp.exp(-v))


def pack_kernel(w1_ref, w2_ref, g_ref, b0, b1, b2, b3, rows_ref):
    x, _ = split()
    w1 = w1_ref[...].astype(F32).T
    w2 = w2_ref[...].astype(F32).T
    for d in range(2):
        t = jnp.swapaxes(g_ref[:, d].astype(F32), 0, 1)
        rows_ref[d, 0] = jnp.zeros((8, W), F32)
        rows_ref[d, 17] = jnp.zeros((8, W), F32)
        rows_ref[d, 1:17] = t
    w1p = jnp.concatenate([w1, jnp.zeros((8, K1P - K1), F32)], axis=1)
    for k, out in enumerate((b0, b1, b2, b3)):
        h0 = xor(x, k) * 4
        parts = [rows_ref[d, h0 + h] for d in range(2) for h in range(6)]
        low = jnp.concatenate([w1p] + parts + [jnp.zeros((8, W), F32)], axis=1)
        out[...] = jnp.concatenate([w2, low], axis=0).astype(BF16)


def group_kernel(b0, b1, b2, b3, w1_ref, w2_ref, go_ref, w2b_ref, top, bot):
    x, _ = split()
    for k, b in enumerate((b0, b1, b2, b3)):
        v = b[...].astype(F32)
        at = rows8(xor(x, k))
        top[at, :] = v[:8]
        bot[at, :] = v[8:]
    w1_ref[...] = bot[:, :K1P].astype(BF16)
    go_ref[...] = bot[:, K1P : K1P + 12 * W].astype(BF16)
    w2_ref[...] = top[...].astype(BF16)
    for j in range(7):
        taps = [top[:, t * W : (t + 1) * W] if t < 27 else jnp.zeros((32, W), F32) for t in range(4 * j, 4 * j + 4)]
        w2b_ref[:, j * W : (j + 1) * W] = jnp.concatenate(taps, axis=0).T.astype(BF16)


def forward_kernel(
    c0, c1, c2, c3, w2_ref, go_ref, xo_ref, xp_ref, xn_ref,
    y_ref, gs0_ref, gs1_ref, slope_ref, xa_ref, xi_ref,
    w1s, zs,
):
    x, zl = split()
    p = lax.axis_index("space")
    for k, c in enumerate((c0, c1, c2, c3)):
        w1s[rows32(xor(zl, k)), :] = c[...]

    def widen(ref, base):
        @pl.loop(0, 20)
        def _(r):
            a, b, c = shifted(ref[r].astype(F32))
            xi_ref[base + r, 0:64] = a.astype(BF16)
            xi_ref[base + r, 64:128] = b.astype(BF16)
            xi_ref[base + r, 128:192] = c.astype(BF16)

    widen(xp_ref, 0)
    widen(xo_ref, 20)
    widen(xn_ref, 40)

    w1 = w1s[:, :K1]

    @pl.loop(0, 16)
    def _(i):
        dd = lax.div(i, 4)
        hh = lax.rem(i, 4) * 2
        cols = []
        for j in range(2):
            cols.append(
                jnp.concatenate(
                    [xi_ref[(dd + a) * 10 + hh + j + b] for a in range(3) for b in range(3)], axis=0
                )
            )
        z = jnp.dot(w1, jnp.concatenate(cols, axis=1), preferred_element_type=F32)
        depth = p * 2 - 1 + dd
        for j in range(2):
            height = x * 4 - 2 + hh + j
            inside = (depth >= 0) & (depth < 16) & (height >= 0) & (height < 16)
            zr = z[:, j * W : (j + 1) * W]
            r = dd * 8 + hh + j
            zs[r] = zr
            act = jnp.where(inside, zr * logistic(zr), 0.0).astype(BF16).astype(F32)
            left, mid, right = shifted(act)
            xa_ref[r, 0:128] = left.astype(BF16)
            xa_ref[r, 128:256] = mid.astype(BF16)
            xa_ref[r, 256:384] = right.astype(BF16)

    for d in range(2):
        for h in range(4):
            v = zs[(d + 1) * 8 + h + 2, rows32(zl), :]
            q = logistic(v)
            slope_ref[:, (d * 4 + h) * W : (d * 4 + h + 1) * W] = q * (1.0 + v * (1.0 - q))

    w2 = w2_ref[...]
    for d in range(2):
        for hp in range(3):
            cols = []
            for j in range(2):
                hh = hp * 2 + j
                cols.append(
                    jnp.concatenate(
                        [xa_ref[(d + a) * 8 + hh + b] for a in range(3) for b in range(3)], axis=0
                    )
                )
            z = jnp.dot(w2, jnp.concatenate(cols, axis=1), preferred_element_type=F32)
            for j in range(2):
                hh = hp * 2 + j
                v = z[:, j * W : (j + 1) * W]
                q = logistic(v)
                if 1 <= hh <= 4:
                    at = (d * 4 + hh - 1) * W
                    y_ref[:, at : at + W] = (v * q).astype(BF16)
                g = go_ref[:, (d * 6 + hh) * W : (d * 6 + hh + 1) * W].astype(F32)
                gs = (g * (q * (1.0 + v * (1.0 - q)))).astype(BF16)
                (gs0_ref if d == 0 else gs1_ref)[hh] = gs


def second_kernel(xa_ref, gs0_ref, gs1_ref, dw_ref):
    gs = jnp.concatenate([(gs0_ref, gs1_ref)[d][h + 1] for d in range(2) for h in range(4)], axis=1)
    for a in range(3):
        for b in range(3):
            col = jnp.concatenate(
                [xa_ref[(d + a) * 8 + h + 1 + b] for d in range(2) for h in range(4)], axis=1
            )
            at = (a * 3 + b) * 384
            dw_ref[:, at : at + 384] = lax.dot_general(gs, col, NT, preferred_element_type=F32)


def back_kernel(gs0_ref, gs1_ref, gp_ref, gn_ref, w2b_ref, own_ref, s1, s2, s3, g3, acc):
    _, zl = split()
    for d, ref in enumerate((gp_ref, gs0_ref, gs1_ref, gn_ref)):
        for h in range(6):
            before, mid, after = shifted(ref[h].astype(F32))
            g3[d * 6 + h, 0:32] = after.astype(BF16)
            g3[d * 6 + h, 32:64] = mid.astype(BF16)
            g3[d * 6 + h, 64:96] = before.astype(BF16)
    w = w2b_ref[...]
    for d in range(2):
        for hp in range(2):
            cols = []
            for j in range(2):
                h = hp * 2 + j
                cols.append(
                    jnp.concatenate(
                        [g3[(d + 2 - a) * 6 + h + 2 - b] for a in range(3) for b in range(3)]
                        + [jnp.zeros((32, W), BF16)],
                        axis=0,
                    )
                )
            at = (d * 4 + hp * 2) * W
            acc[:, at : at + 2 * W] = jnp.dot(w, jnp.concatenate(cols, axis=1), preferred_element_type=F32)
    own_ref[...] = acc[rows32(zl), :]
    for k, out in enumerate((s1, s2, s3)):
        out[...] = acc[rows32(xor(zl, k + 1)), :].astype(BF16)


def first_kernel(own_ref, r1, r2, r3, slope_ref, xi_ref, dw2_ref, y_ref, o0, s1, s2, s3, low):
    x, _ = split()
    back = (own_ref[...] + r1[...].astype(F32)) + (r2[...].astype(F32) + r3[...].astype(F32))
    gf = (back * slope_ref[...]).astype(BF16)
    parts = []
    for a in range(3):
        col = jnp.concatenate(
            [
                jnp.concatenate(
                    [xi_ref[(d + 1 + a) * 10 + h + 2 + b] for d in range(2) for h in range(4)], axis=1
                )
                for b in range(3)
            ],
            axis=0,
        )
        parts.append(lax.dot_general(gf, col, NT, preferred_element_type=F32))
    low[:, :K1P] = jnp.concatenate(parts + [jnp.zeros((32, K1P - K1), F32)], axis=1)
    low[:, K1P : K1P + 1024] = y_ref[...].astype(F32)
    low[:, K1P + 1024 :] = jnp.zeros((32, K2 - K1P - 1024), F32)
    for k, out in enumerate((o0, s1, s2, s3)):
        at = rows8(xor(x, k))
        both = jnp.concatenate([dw2_ref[at, :], low[at, :]], axis=0)
        out[...] = both.astype(out.dtype)


def sum_kernel(o0, r1, r2, r3, dw_ref, y_ref):
    x, _ = split()
    parts = [o0[...], r1[...].astype(F32), r2[...].astype(F32), r3[...].astype(F32)]
    total = (parts[0] + parts[1]) + (parts[2] + parts[3])
    flat = jnp.concatenate([total[:8], total[8:, :K1P], jnp.zeros((8, W), F32)], axis=1)
    dw_ref[...] = jnp.concatenate([flat[:, :2688], flat[:, 2688:]], axis=0).astype(BF16)
    for k, v in enumerate(parts):
        h0 = xor(x, k) * 4
        for d in range(2):
            for h in range(4):
                at = K1P + (d * 4 + h) * W
                y_ref[d, h0 + h] = v[8:, at : at + W]


def last_kernel(a0, a1, a2, a3, dw1_ref, dw2_ref):
    v = [a[...].astype(F32) for a in (a0, a1, a2, a3)]
    total = ((v[0] + v[1]) + (v[2] + v[3])) * (1.0 / 256.0)
    top = total[:8].T
    bot = total[8:].T
    dw2_ref[:2688] = top
    dw2_ref[2688:] = bot[: K2 - 2688]
    dw1_ref[...] = bot[K2 - 2688 : K2 - 2688 + K1]


def local(act_in, w_first, w_second, grad_out):
    X = [[(z * 4 + x, z * 4 + (x ^ k)) for z in range(4) for x in range(4)] for k in range(4)]
    Z = [[(z * 4 + x, (z ^ k) * 4 + x) for z in range(4) for x in range(4)] for k in range(4)]
    up = [(i, i + 1) for i in range(7)]
    down = [(i + 1, i) for i in range(7)]
    x = lax.rem(lax.axis_index("filt"), 4)

    b = run(
        pack_kernel,
        [sds((16, K2), BF16)] * 4,
        [w_first.reshape(K1, 8), w_second.reshape(K2, 8), grad_out[0]],
        [pltpu.VMEM((2, 18, 8, W), F32)],
    )
    b = [b[0]] + [lax.ppermute(b[k], "filt", X[k]) for k in (1, 2, 3)]

    rows = jnp.pad(jnp.transpose(act_in[0], (1, 2, 0, 3)), ((0, 0), (3, 3), (0, 0), (0, 0)))
    xo = lax.dynamic_slice_in_dim(rows, x * 4, 10, axis=1).reshape(20, 64, W)
    xp = lax.ppermute(xo, "space", up)
    xn = lax.ppermute(xo, "space", down)

    w1, w2, go, w2b = run(
        group_kernel,
        [sds((32, K1P), BF16), sds((32, K2), BF16), sds((32, 12 * W), BF16), sds((128, KB), BF16)],
        b,
        [pltpu.VMEM((32, K2), F32), pltpu.VMEM((32, K2), F32)],
    )
    c = [w1] + [lax.ppermute(w1, "filt", Z[k]) for k in (1, 2, 3)]

    y, gs0, gs1, slope, xa, xi = run(
        forward_kernel,
        [
            sds((32, 1024), BF16),
            sds((6, 32, W), BF16),
            sds((6, 32, W), BF16),
            sds((32, 1024), F32),
            sds((32, 384, W), BF16),
            sds((60, 192, W), BF16),
        ],
        c + [w2, go, xo, xp, xn],
        [pltpu.VMEM((128, K1P), BF16), pltpu.VMEM((32, 128, W), F32)],
    )
    gp = lax.ppermute(gs1, "space", up)
    gn = lax.ppermute(gs0, "space", down)
    (dw2,) = run(second_kernel, [sds((32, K2), F32)], [xa, gs0, gs1])

    own, *s = run(
        back_kernel,
        [sds((32, 1024), F32)] + [sds((32, 1024), BF16)] * 3,
        [gs0, gs1, gp, gn, w2b],
        [pltpu.VMEM((24, 96, W), BF16), pltpu.VMEM((128, 1024), F32)],
    )
    s = [lax.ppermute(s[k - 1], "filt", Z[k]) for k in (1, 2, 3)]

    o, *s = run(
        first_kernel,
        [sds((16, K2), F32)] + [sds((16, K2), BF16)] * 3,
        [own] + s + [slope, xi, dw2, y],
        [pltpu.VMEM((32, K2), F32)],
    )
    s = [lax.ppermute(s[k - 1], "filt", X[k]) for k in (1, 2, 3)]
    part, yt = run(sum_kernel, [sds((16, 2688), BF16), sds((2, 16, 8, W), F32)], [o] + s)
    y_out = jnp.transpose(yt, (2, 0, 1, 3)).astype(BF16)[None]

    def pair(ds, dc):
        return [(s * 8 + i, (s ^ ds) * 8 + (i ^ dc)) for s in range(2) for i in range(8)]

    both = ("sample", "space")
    q = [part] + [lax.ppermute(part, both, pair(ds, dc)) for ds, dc in ((0, 1), (1, 0), (1, 1))]
    q = [v.astype(F32) for v in q]
    part = ((q[0] + q[1]) + (q[2] + q[3])).astype(BF16)
    q = [part] + [lax.ppermute(part, "space", [(i, i ^ (2 * k)) for i in range(8)]) for k in (1, 2, 3)]
    dw1, dw2 = run(last_kernel, [sds((K1, 8), F32), sds((K2, 8), F32)], q)
    return y_out, dw1.reshape(27, 64, 8), dw2.reshape(27, 128, 8)


def solution(mesh):
    placed = (
        P("sample", None, "space", None, None),
        P(None, None, "filt"),
        P(None, None, "filt"),
        P("sample", "filt", "space", None, None),
    )
    return jax.shard_map(
        local,
        mesh=mesh,
        in_specs=placed,
        out_specs=(
            P("sample", "filt", "space", None, None),
            P(None, None, "filt"),
            P(None, None, "filt"),
        ),
        check_vma=False,
    )
```

```python
import jax
import jax.numpy as jnp
from jax import lax
from jax.experimental import pallas as pl
from jax.experimental.pallas import tpu as pltpu
from jax.sharding import PartitionSpec as P

F32 = jnp.float32
BF16 = jnp.bfloat16
W = 128
K1, K2 = 27 * 64, 27 * 128
K1P = 1792
K1H = 896
HALF = 2688
KB = 896
VMEM = pl.BlockSpec(memory_space=pltpu.VMEM)
NT = (((1,), (1,)), ((), ()))


def run(kernel, outs, args, scratch=(), flops=10**8):
    return pl.pallas_call(
        kernel,
        out_shape=outs,
        in_specs=[VMEM] * len(args),
        out_specs=[VMEM] * len(outs),
        scratch_shapes=list(scratch),
        cost_estimate=pl.CostEstimate(flops=flops, bytes_accessed=10**5, transcendentals=0),
        compiler_params=pltpu.CompilerParams(vmem_limit_bytes=20 * 1024 * 1024),
    )(*args)


def sds(shape, dtype):
    return jax.ShapeDtypeStruct(shape, dtype)


def split():
    f = lax.axis_index("filt")
    return lax.rem(f, 4), lax.div(f, 4)


def xor(a, k):
    return lax.bitwise_xor(a, jnp.int32(k))


def rows8(i):
    return pl.ds(pl.multiple_of(i * 8, 8), 8)


def rows32(i):
    return pl.ds(pl.multiple_of(i * 32, 32), 32)


def lanes(core):
    return pl.ds(pl.multiple_of(core * HALF, W), HALF)


def shifted(x):
    lane = lax.broadcasted_iota(jnp.int32, x.shape, 1)
    left = jnp.where(lane == 0, 0.0, pltpu.roll(x, 1, 1))
    right = jnp.where(lane == W - 1, 0.0, pltpu.roll(x, W - 1, 1))
    return left, x, right


def logistic(v):
    return 0.5 * jnp.tanh(0.5 * v) + 0.5


def pack_first_kernel(w1_ref, out, acc):
    core = lax.rem(lax.axis_index("space"), 2)
    w1 = [w1_ref[t].astype(F32) for t in range(27)]
    acc[...] = jnp.concatenate(w1 + [jnp.zeros((8, K1P - K1), F32)], axis=1)
    out[...] = acc[:, pl.ds(pl.multiple_of(core * K1H, W), K1H)].astype(BF16)


def pack_second_kernel(w2_ref, g_ref, b0, b1, b2, b3, rows_ref):
    x, _ = split()
    w2 = [w2_ref[t].astype(F32) for t in range(27)]
    for d in range(2):
        t = jnp.swapaxes(g_ref[:, d].astype(F32), 0, 1)
        rows_ref[d, 0] = jnp.zeros((8, W), F32)
        rows_ref[d, 17] = jnp.zeros((8, W), F32)
        rows_ref[d, 1:17] = t
    for k, out in enumerate((b0, b1, b2, b3)):
        h0 = xor(x, k) * 4
        parts = [rows_ref[d, h0 + h] for d in range(2) for h in range(6)]
        out[...] = jnp.concatenate(w2 + parts, axis=1).astype(BF16)


def stack_kernel(b0, b1, b2, b3, w1_ref, acc):
    _, zl = split()
    for k, b in enumerate((b0, b1, b2, b3)):
        acc[rows8(xor(zl, k)), :] = b[...].astype(F32)
    w1_ref[...] = acc[...].astype(BF16)


def order_kernel(c0, c1, c2, c3, w1_ref, acc):
    x, _ = split()
    for k, c in enumerate((c0, c1, c2, c3)):
        v = c[...].astype(F32)
        for z in range(4):
            acc[rows8(z * 4 + xor(x, k)), :] = v[z * 8 : z * 8 + 8]
    w1_ref[...] = acc[...].astype(BF16)


def widen_kernel(xo_ref, xp_ref, xn_ref, xi_ref):
    p = lax.axis_index("space")
    for base, ref, inside in ((0, xp_ref, p > 0), (20, xo_ref, None), (40, xn_ref, p < 7)):
        for r in range(20):
            v = ref[r].astype(F32)
            a, b, c = shifted(v if inside is None else jnp.where(inside, v, 0.0))
            xi_ref[base + r, 0:64] = a.astype(BF16)
            xi_ref[base + r, 64:128] = b.astype(BF16)
            xi_ref[base + r, 128:192] = c.astype(BF16)


def conv_first_kernel(own_ref, got_ref, xi_ref, slope_ref, xa_ref, zs):
    x, zl = split()
    p = lax.axis_index("space")
    own, got = own_ref[...], got_ref[...]
    first = lax.rem(p, 2) == 0
    w1 = jnp.concatenate([jnp.where(first, own, got), jnp.where(first, got, own)], axis=1)[:, :K1]

    for i in range(16):
        dd, hh = i // 4, i % 4 * 2
        cols = []
        for j in range(2):
            cols.append(
                jnp.concatenate(
                    [xi_ref[(dd + a) * 10 + hh + j + b] for a in range(3) for b in range(3)], axis=0
                )
            )
        z = jnp.dot(w1, jnp.concatenate(cols, axis=1), preferred_element_type=F32)
        depth = p * 2 - 1 + dd
        for j in range(2):
            height = x * 4 - 2 + hh + j
            inside = (depth >= 0) & (depth < 16) & (height >= 0) & (height < 16)
            zr = z[:, j * W : (j + 1) * W]
            r = dd * 8 + hh + j
            zs[r] = zr
            act = jnp.where(inside, zr * logistic(zr), 0.0).astype(BF16).astype(F32)
            left, mid, right = shifted(act)
            xa_ref[r, 0:128] = left.astype(BF16)
            xa_ref[r, 128:256] = mid.astype(BF16)
            xa_ref[r, 256:384] = right.astype(BF16)

    for d in range(2):
        for h in range(4):
            v = zs[(d + 1) * 8 + h + 2, rows32(zl), :]
            q = logistic(v)
            slope_ref[:, (d * 4 + h) * W : (d * 4 + h + 1) * W] = q * (1.0 + v * (1.0 - q))


def conv_second_kernel(b0, b1, b2, b3, xa_ref, y_ref, gs0_ref, gs1_ref, w2b_ref, acc, w2_ref):
    x, _ = split()
    for k, b in enumerate((b0, b1, b2, b3)):
        acc[rows8(xor(x, k)), :] = b[...].astype(F32)
    w2_ref[...] = acc[:, :K2].astype(BF16)
    for j in range(7):
        taps = [acc[:, t * W : (t + 1) * W] if t < 27 else jnp.zeros((32, W), F32) for t in range(4 * j, 4 * j + 4)]
        w2b_ref[:, j * W : (j + 1) * W] = jnp.concatenate(taps, axis=0).T.astype(BF16)
    planes = [[], []]
    for dd in range(4):
        taps = [a for a in range(3) if 0 <= dd - a <= 1]
        w = jnp.concatenate(
            [w2_ref[:, t * 384 : (t + 1) * 384] for a in taps for t in range(3 * a, 3 * a + 3)], axis=0
        )
        col = jnp.concatenate([xa_ref[dd * 8 + h] for h in range(8)], axis=1)
        part = jnp.dot(w, col, preferred_element_type=F32)
        for k, a in enumerate(taps):
            for b in range(3):
                at = (k * 3 + b) * 32
                planes[dd - a].append(part[at : at + 32, b * W : (b + 6) * W])
    for d in range(2):
        t = planes[d]
        z = ((t[0] + t[1]) + (t[2] + t[3])) + ((t[4] + t[5]) + (t[6] + t[7])) + t[8]
        for hh in range(6):
            v = z[:, hh * W : (hh + 1) * W]
            q = logistic(v)
            if 1 <= hh <= 4:
                at = (d * 4 + hh - 1) * W
                y_ref[:, at : at + W] = (v * q).astype(BF16)
            g = acc[:, K2 + (d * 6 + hh) * W : K2 + (d * 6 + hh + 1) * W]
            gs = (g * (q * (1.0 + v * (1.0 - q)))).astype(BF16)
            (gs0_ref if d == 0 else gs1_ref)[hh] = gs


def second_kernel(xa_ref, gs0_ref, gs1_ref, dw_ref):
    gs = jnp.concatenate([(gs0_ref, gs1_ref)[d][h + 1] for d in range(2) for h in range(4)], axis=1)
    for a in range(3):
        for b in range(3):
            col = jnp.concatenate(
                [xa_ref[(d + a) * 8 + h + 1 + b] for d in range(2) for h in range(4)], axis=1
            )
            at = (a * 3 + b) * 384
            dw_ref[:, at : at + 384] = lax.dot_general(gs, col, NT, preferred_element_type=F32)


def back_kernel(gs0_ref, gs1_ref, gp_ref, gn_ref, w2b_ref, own_ref, s1, s2, s3, g3, acc):
    _, zl = split()
    p = lax.axis_index("space")
    sides = ((gp_ref, p > 0), (gs0_ref, None), (gs1_ref, None), (gn_ref, p < 7))
    for d, (ref, inside) in enumerate(sides):
        for h in range(6):
            v = ref[h].astype(F32)
            before, mid, after = shifted(v if inside is None else jnp.where(inside, v, 0.0))
            g3[d * 6 + h, 0:32] = after.astype(BF16)
            g3[d * 6 + h, 32:64] = mid.astype(BF16)
            g3[d * 6 + h, 64:96] = before.astype(BF16)
    w = w2b_ref[...]
    for d in range(2):
        for hp in range(2):
            cols = []
            for j in range(2):
                h = hp * 2 + j
                cols.append(
                    jnp.concatenate(
                        [g3[(d + 2 - a) * 6 + h + 2 - b] for a in range(3) for b in range(3)]
                        + [jnp.zeros((32, W), BF16)],
                        axis=0,
                    )
                )
            at = (d * 4 + hp * 2) * W
            acc[:, at : at + 2 * W] = jnp.dot(w, jnp.concatenate(cols, axis=1), preferred_element_type=F32)
    own_ref[...] = acc[rows32(zl), :]
    for k, out in enumerate((s1, s2, s3)):
        out[...] = acc[rows32(xor(zl, k + 1)), :].astype(BF16)


def first_kernel(own_ref, r1, r2, r3, slope_ref, xi_ref, dw2_ref, keep_ref, give_ref, acc):
    core = lax.rem(lax.axis_index("space"), 2)
    back = (own_ref[...] + r1[...].astype(F32)) + (r2[...].astype(F32) + r3[...].astype(F32))
    gf = (back * slope_ref[...]).astype(BF16)
    parts = []
    for a in range(3):
        col = jnp.concatenate(
            [
                jnp.concatenate(
                    [xi_ref[(d + 1 + a) * 10 + h + 2 + b] for d in range(2) for h in range(4)], axis=1
                )
                for b in range(3)
            ],
            axis=0,
        )
        parts.append(lax.dot_general(gf, col, NT, preferred_element_type=F32))
    acc[:, :K2] = dw2_ref[...]
    acc[:, K2:] = jnp.concatenate(parts + [jnp.zeros((32, 2 * HALF - K2 - K1), F32)], axis=1)
    keep_ref[...] = acc[:, lanes(core)]
    give_ref[...] = acc[:, lanes(1 - core)]


def chip_kernel(keep_ref, got_ref, y_ref, o0, y0, s1, s2, s3, acc, yacc):
    x, _ = split()
    acc[...] = keep_ref[...] + got_ref[...]
    yacc[...] = y_ref[...].astype(F32)
    o0[...] = acc[rows8(x), :]
    y0[...] = yacc[rows8(x), :]
    for k, out in enumerate((s1, s2, s3)):
        at = rows8(xor(x, k + 1))
        out[...] = jnp.concatenate([acc[at, :], yacc[at, :]], axis=1).astype(BF16)


def sum_kernel(o0, y0, r1, r2, r3, dw_ref, y_ref):
    x, _ = split()
    parts = [r[...].astype(F32) for r in (r1, r2, r3)]
    dw_ref[...] = ((o0[...] + parts[0][:, :HALF]) + (parts[1][:, :HALF] + parts[2][:, :HALF])).astype(BF16)
    for k, v in enumerate([y0[...]] + [r[:, HALF:] for r in parts]):
        h0 = xor(x, k) * 4
        for d in range(2):
            for h in range(4):
                at = (d * 4 + h) * W
                y_ref[d, h0 + h] = v[:, at : at + W]


def last_kernel(own_ref, got_ref, dw1_ref, dw2_ref):
    core = lax.rem(lax.axis_index("space"), 2)
    own, got = own_ref[...], got_ref[...]
    both = [jnp.where(core == 0, own, got), jnp.where(core == 0, got, own)]
    both = jnp.concatenate(both, axis=1) * (1.0 / 256.0)
    for t in range(27):
        dw2_ref[t] = both[:, t * W : (t + 1) * W]
        dw1_ref[t] = both[:, K2 + t * 64 : K2 + (t + 1) * 64]


def local(act_in, w_first, w_second, grad_out):
    X = [[(z * 4 + x, z * 4 + (x ^ k)) for z in range(4) for x in range(4)] for k in range(4)]
    Z = [[(z * 4 + x, (z ^ k) * 4 + x) for z in range(4) for x in range(4)] for k in range(4)]
    up = [(i, (i + 1) % 8) for i in range(8)]
    down = [((i + 1) % 8, i) for i in range(8)]
    other = [(i, i ^ 1) for i in range(8)]
    x = lax.rem(lax.axis_index("filt"), 4)

    (w0,) = run(
        pack_first_kernel,
        [sds((8, K1H), BF16)],
        [jnp.transpose(w_first, (0, 2, 1))],
        [pltpu.VMEM((8, K1P), F32)],
    )
    c = [w0] + [lax.ppermute(w0, "filt", Z[k]) for k in (1, 2, 3)]
    act_in, w0 = lax.optimization_barrier((act_in, w0))
    w_second, grad_out, w0 = lax.optimization_barrier((w_second, grad_out, w0))
    rows = jnp.pad(jnp.transpose(act_in[0], (1, 2, 0, 3)), ((0, 0), (3, 3), (0, 0), (0, 0)))
    xo = lax.dynamic_slice_in_dim(rows, x * 4, 10, axis=1).reshape(20, 64, W)
    xp = lax.ppermute(xo, "space", up)
    xn = lax.ppermute(xo, "space", down)

    (w1,) = run(stack_kernel, [sds((32, K1H), BF16)], c, [pltpu.VMEM((32, K1H), F32)])
    c = [w1] + [lax.ppermute(w1, "filt", X[k]) for k in (1, 2, 3)]
    b = run(
        pack_second_kernel,
        [sds((8, K2 + 12 * W), BF16)] * 4,
        [jnp.transpose(w_second, (0, 2, 1)), grad_out[0]],
        [pltpu.VMEM((2, 18, 8, W), F32)],
    )
    b, c = lax.optimization_barrier((b, c))
    (w1,) = run(order_kernel, [sds((128, K1H), BF16)], c, [pltpu.VMEM((128, K1H), F32)])
    w1got = lax.ppermute(w1, "space", other)

    b, w1 = lax.optimization_barrier((b, w1))
    b = [b[0]] + [lax.ppermute(b[k], "filt", X[k]) for k in (1, 2, 3)]
    (xi,) = run(widen_kernel, [sds((60, 192, W), BF16)], [xo, xp, xn], flops=8 * 10**8)
    slope, xa = run(
        conv_first_kernel,
        [sds((32, 1024), F32), sds((32, 384, W), BF16)],
        [w1, w1got, xi],
        [pltpu.VMEM((32, 128, W), F32)],
        4 * 10**9,
    )
    y, gs0, gs1, w2b = run(
        conv_second_kernel,
        [sds((32, 1024), BF16), sds((6, 32, W), BF16), sds((6, 32, W), BF16), sds((128, KB), BF16)],
        b + [xa],
        [pltpu.VMEM((32, K2 + 12 * W), F32), pltpu.VMEM((32, K2), BF16)],
    )
    gp = lax.ppermute(gs1, "space", up)
    gn = lax.ppermute(gs0, "space", down)
    (dw2,) = run(second_kernel, [sds((32, K2), F32)], [xa, gs0, gs1], flops=25 * 10**8)

    own, *s = run(
        back_kernel,
        [sds((32, 1024), F32)] + [sds((32, 1024), BF16)] * 3,
        [gs0, gs1, gp, gn, w2b],
        [pltpu.VMEM((24, 96, W), BF16), pltpu.VMEM((128, 1024), F32)],
    )
    s = [lax.ppermute(s[k - 1], "filt", Z[k]) for k in (1, 2, 3)]

    keep, give = run(
        first_kernel,
        [sds((32, HALF), F32)] * 2,
        [own] + s + [slope, xi, dw2],
        [pltpu.VMEM((32, 2 * HALF), F32)],
    )
    got = lax.ppermute(give, "space", other)
    o, yo, *s = run(
        chip_kernel,
        [sds((8, HALF), F32), sds((8, 1024), F32)] + [sds((8, HALF + 1024), BF16)] * 3,
        [keep, got, y],
        [pltpu.VMEM((32, HALF), F32), pltpu.VMEM((32, 1024), F32)],
    )
    s = [lax.ppermute(s[k - 1], "filt", X[k]) for k in (1, 2, 3)]
    part, yt = run(sum_kernel, [sds((8, HALF), BF16), sds((2, 16, 8, W), F32)], [o, yo] + s)
    y_out = jnp.transpose(yt, (2, 0, 1, 3)).astype(BF16)[None]

    q = [part] + [lax.ppermute(part, "space", [(i, i ^ (2 * k)) for i in range(8)]) for k in (1, 2, 3)]
    q = [v.astype(F32) for v in q]
    part = ((q[0] + q[1]) + (q[2] + q[3])).astype(BF16)
    part = part.astype(F32) + lax.ppermute(part, "sample", [(0, 1), (1, 0)]).astype(F32)
    got = lax.ppermute(part, "space", other)
    dw1, dw2 = run(last_kernel, [sds((27, 8, 64), F32), sds((27, 8, 128), F32)], [part, got])
    return y_out, jnp.transpose(dw1, (0, 2, 1)), jnp.transpose(dw2, (0, 2, 1))


def solution(mesh):
    placed = (
        P("sample", None, "space", None, None),
        P(None, None, "filt"),
        P(None, None, "filt"),
        P("sample", "filt", "space", None, None),
    )
    return jax.shard_map(
        local,
        mesh=mesh,
        in_specs=placed,
        out_specs=(
            P("sample", "filt", "space", None, None),
            P(None, None, "filt"),
            P(None, None, "filt"),
        ),
        check_vma=False,
    )
```

```python
import jax
import jax.numpy as jnp
from jax import lax
from jax.experimental import pallas as pl
from jax.experimental.pallas import tpu as pltpu
from jax.sharding import PartitionSpec as P

F32 = jnp.float32
BF16 = jnp.bfloat16
W = 128
K1, K2 = 27 * 64, 27 * 128
K1P = 1792
HALF = 2688
KB = 896
VMEM = pl.BlockSpec(memory_space=pltpu.VMEM)
NT = (((1,), (1,)), ((), ()))


def run(kernel, outs, args, scratch=(), flops=10**8):
    return pl.pallas_call(
        kernel,
        out_shape=outs,
        in_specs=[VMEM] * len(args),
        out_specs=[VMEM] * len(outs),
        scratch_shapes=list(scratch),
        cost_estimate=pl.CostEstimate(flops=flops, bytes_accessed=10**5, transcendentals=0),
        compiler_params=pltpu.CompilerParams(vmem_limit_bytes=20 * 1024 * 1024),
    )(*args)


def sds(shape, dtype):
    return jax.ShapeDtypeStruct(shape, dtype)


def split():
    f = lax.axis_index("filt")
    return lax.rem(f, 4), lax.div(f, 4)


def xor(a, k):
    return lax.bitwise_xor(a, jnp.int32(k))


def rows8(i):
    return pl.ds(pl.multiple_of(i * 8, 8), 8)


def rows32(i):
    return pl.ds(pl.multiple_of(i * 32, 32), 32)


def lanes(core):
    return pl.ds(pl.multiple_of(core * HALF, W), HALF)


def shifted(x):
    lane = lax.broadcasted_iota(jnp.int32, x.shape, 1)
    left = jnp.where(lane == 0, 0.0, pltpu.roll(x, 1, 1))
    right = jnp.where(lane == W - 1, 0.0, pltpu.roll(x, W - 1, 1))
    return left, x, right


def logistic(v):
    return 0.5 * jnp.tanh(0.5 * v) + 0.5


def pack_first_kernel(w1_ref, out):
    w1 = [w1_ref[t].astype(F32) for t in range(27)]
    out[...] = jnp.concatenate(w1 + [jnp.zeros((8, K1P - K1), F32)], axis=1).astype(BF16)


def prepare_kernel(w2_ref, g_ref, b0, b1, b2, b3, rows_ref, acc):
    x, _ = split()
    core = lax.rem(lax.axis_index("space"), 2)
    for t in range(27):
        acc[:, t * W : (t + 1) * W] = w2_ref[t].astype(F32)
    w2 = acc[:, pl.ds(pl.multiple_of(core * (13 * W), W), K1P)]
    for d in range(2):
        t = jnp.swapaxes(g_ref[:, d].astype(F32), 0, 1)
        rows_ref[d, 0] = jnp.zeros((8, W), F32)
        rows_ref[d, 17] = jnp.zeros((8, W), F32)
        rows_ref[d, 1:17] = t
    for k, out in enumerate((b0, b1, b2, b3)):
        h0 = xor(x, k) * 4
        parts = [rows_ref[d, h0 + h] for d in range(2) for h in range(6)]
        out[...] = jnp.concatenate([w2] + parts, axis=1).astype(BF16)


def pack_kernel(w0_ref, p1_ref, p2_ref, a0, a1, a2, a3, b0, b1, b2, b3):
    _, zl = split()
    core = lax.rem(lax.axis_index("space"), 2)
    w0, p1, p2 = w0_ref[...], p1_ref[...], p2_ref[...]
    same, other = jnp.where(core == 0, w0, p1), jnp.where(core == 0, p1, p2)
    even = lax.rem(zl, 2) == 0
    low, high = jnp.where(even, same, other), jnp.where(even, other, same)
    for a, b in zip((a0, a1, a2, a3), (b0, b1, b2, b3)):
        b[:, :K1P] = low
        b[:, K1P : 2 * K1P] = high
        b[:, 2 * K1P :] = a[...]


def order_kernel(b0, b1, b2, b3, half_ref, go_ref, acc, acc_go):
    x, _ = split()
    for k, b in enumerate((b0, b1, b2, b3)):
        v = b[...].astype(F32)
        for j in range(3):
            acc[rows8(j * 4 + xor(x, k)), :] = v[:, j * K1P : (j + 1) * K1P]
        acc_go[rows8(xor(x, k)), :] = v[:, 3 * K1P :]
    half_ref[...] = acc[...].astype(BF16)
    go_ref[...] = acc_go[...].astype(BF16)


def widen_kernel(xo_ref, xp_ref, xn_ref, xi_ref):
    p = lax.axis_index("space")
    for base, ref, inside in ((0, xp_ref, p > 0), (20, xo_ref, None), (40, xn_ref, p < 7)):
        for r in range(20):
            v = ref[r].astype(F32)
            a, b, c = shifted(v if inside is None else jnp.where(inside, v, 0.0))
            xi_ref[base + r, 0:64] = a.astype(BF16)
            xi_ref[base + r, 64:128] = b.astype(BF16)
            xi_ref[base + r, 128:192] = c.astype(BF16)


def conv_first_kernel(own_ref, got_ref, xi_ref, slope_ref, xa_ref, zs):
    x, zl = split()
    p = lax.axis_index("space")
    own, got = own_ref[:64], got_ref[:64]
    first = lax.rem(lax.div(zl, 2) + p, 2) == 0
    w1 = jnp.concatenate([jnp.where(first, own, got), jnp.where(first, got, own)], axis=0)[:, :K1]

    for i in range(16):
        dd, hh = i // 4, i % 4 * 2
        cols = []
        for j in range(2):
            cols.append(
                jnp.concatenate(
                    [xi_ref[(dd + a) * 10 + hh + j + b] for a in range(3) for b in range(3)], axis=0
                )
            )
        z = jnp.dot(w1, jnp.concatenate(cols, axis=1), preferred_element_type=F32)
        depth = p * 2 - 1 + dd
        for j in range(2):
            height = x * 4 - 2 + hh + j
            inside = (depth >= 0) & (depth < 16) & (height >= 0) & (height < 16)
            zr = z[:, j * W : (j + 1) * W]
            r = dd * 8 + hh + j
            zs[r] = zr
            act = jnp.where(inside, zr * logistic(zr), 0.0).astype(BF16).astype(F32)
            left, mid, right = shifted(act)
            xa_ref[r, 0:128] = left.astype(BF16)
            xa_ref[r, 128:256] = mid.astype(BF16)
            xa_ref[r, 256:384] = right.astype(BF16)

    for d in range(2):
        for h in range(4):
            v = zs[(d + 1) * 8 + h + 2, rows32(zl), :]
            q = logistic(v)
            slope_ref[:, (d * 4 + h) * W : (d * 4 + h + 1) * W] = q * (1.0 + v * (1.0 - q))


def conv_second_kernel(own_ref, got_ref, go_ref, xa_ref, y_ref, gs0_ref, gs1_ref, w2b_ref, acc, w2_ref):
    first = lax.rem(lax.axis_index("space"), 2) == 0
    own, got = own_ref[64:], got_ref[64:]
    w2_ref[:, : 14 * W] = jnp.where(first, own, got)
    w2_ref[:, 14 * W :] = jnp.where(first, got, own)[:, W:]
    acc[...] = w2_ref[...].astype(F32)
    for j in range(7):
        taps = [acc[:, t * W : (t + 1) * W] if t < 27 else jnp.zeros((32, W), F32) for t in range(4 * j, 4 * j + 4)]
        w2b_ref[:, j * W : (j + 1) * W] = jnp.concatenate(taps, axis=0).T.astype(BF16)
    planes = [[], []]
    for dd in range(4):
        taps = [a for a in range(3) if 0 <= dd - a <= 1]
        w = jnp.concatenate(
            [w2_ref[:, t * 384 : (t + 1) * 384] for a in taps for t in range(3 * a, 3 * a + 3)], axis=0
        )
        col = jnp.concatenate([xa_ref[dd * 8 + h] for h in range(8)], axis=1)
        part = jnp.dot(w, col, preferred_element_type=F32)
        for k, a in enumerate(taps):
            for b in range(3):
                at = (k * 3 + b) * 32
                planes[dd - a].append(part[at : at + 32, b * W : (b + 6) * W])
    for d in range(2):
        t = planes[d]
        z = ((t[0] + t[1]) + (t[2] + t[3])) + ((t[4] + t[5]) + (t[6] + t[7])) + t[8]
        for hh in range(6):
            v = z[:, hh * W : (hh + 1) * W]
            q = logistic(v)
            if 1 <= hh <= 4:
                at = (d * 4 + hh - 1) * W
                y_ref[:, at : at + W] = (v * q).astype(BF16)
            g = go_ref[:, (d * 6 + hh) * W : (d * 6 + hh + 1) * W].astype(F32)
            gs = (g * (q * (1.0 + v * (1.0 - q)))).astype(BF16)
            (gs0_ref if d == 0 else gs1_ref)[hh] = gs


def second_kernel(xa_ref, gs0_ref, gs1_ref, dw_ref):
    gs = jnp.concatenate([(gs0_ref, gs1_ref)[d][h + 1] for d in range(2) for h in range(4)], axis=1)
    for a in range(3):
        for b in range(3):
            col = jnp.concatenate(
                [xa_ref[(d + a) * 8 + h + 1 + b] for d in range(2) for h in range(4)], axis=1
            )
            at = (a * 3 + b) * 384
            dw_ref[:, at : at + 384] = lax.dot_general(gs, col, NT, preferred_element_type=F32)


def back_kernel(gs0_ref, gs1_ref, gp_ref, gn_ref, w2b_ref, own_ref, s1, s2, s3, g3, acc):
    _, zl = split()
    p = lax.axis_index("space")
    sides = ((gp_ref, p > 0), (gs0_ref, None), (gs1_ref, None), (gn_ref, p < 7))
    for d, (ref, inside) in enumerate(sides):
        for h in range(6):
            v = ref[h].astype(F32)
            before, mid, after = shifted(v if inside is None else jnp.where(inside, v, 0.0))
            g3[d * 6 + h, 0:32] = after.astype(BF16)
            g3[d * 6 + h, 32:64] = mid.astype(BF16)
            g3[d * 6 + h, 64:96] = before.astype(BF16)
    w = w2b_ref[...]
    for d in range(2):
        for hp in range(2):
            cols = []
            for j in range(2):
                h = hp * 2 + j
                cols.append(
                    jnp.concatenate(
                        [g3[(d + 2 - a) * 6 + h + 2 - b] for a in range(3) for b in range(3)]
                        + [jnp.zeros((32, W), BF16)],
                        axis=0,
                    )
                )
            at = (d * 4 + hp * 2) * W
            acc[:, at : at + 2 * W] = jnp.dot(w, jnp.concatenate(cols, axis=1), preferred_element_type=F32)
    own_ref[...] = acc[rows32(zl), :]
    for k, out in enumerate((s1, s2, s3)):
        out[...] = acc[rows32(xor(zl, k + 1)), :].astype(BF16)


def first_kernel(own_ref, r1, r2, r3, slope_ref, xi_ref, dw2_ref, keep_ref, give_ref, acc):
    core = lax.rem(lax.axis_index("space"), 2)
    back = (own_ref[...] + r1[...].astype(F32)) + (r2[...].astype(F32) + r3[...].astype(F32))
    gf = (back * slope_ref[...]).astype(BF16)
    parts = []
    for a in range(3):
        col = jnp.concatenate(
            [
                jnp.concatenate(
                    [xi_ref[(d + 1 + a) * 10 + h + 2 + b] for d in range(2) for h in range(4)], axis=1
                )
                for b in range(3)
            ],
            axis=0,
        )
        parts.append(lax.dot_general(gf, col, NT, preferred_element_type=F32))
    acc[:, :K2] = dw2_ref[...]
    acc[:, K2:] = jnp.concatenate(parts + [jnp.zeros((32, 2 * HALF - K2 - K1), F32)], axis=1)
    keep_ref[...] = acc[:, lanes(core)]
    give_ref[...] = acc[:, lanes(1 - core)]


def chip_kernel(keep_ref, got_ref, y_ref, o0, y0, s1, s2, s3, acc, yacc):
    x, _ = split()
    acc[...] = keep_ref[...] + got_ref[...]
    yacc[...] = y_ref[...].astype(F32)
    o0[...] = acc[rows8(x), :]
    y0[...] = yacc[rows8(x), :]
    for k, out in enumerate((s1, s2, s3)):
        at = rows8(xor(x, k + 1))
        out[...] = jnp.concatenate([acc[at, :], yacc[at, :]], axis=1).astype(BF16)


def sum_kernel(o0, y0, r1, r2, r3, dw_ref, y_ref):
    x, _ = split()
    parts = [r[...].astype(F32) for r in (r1, r2, r3)]
    dw_ref[...] = ((o0[...] + parts[0][:, :HALF]) + (parts[1][:, :HALF] + parts[2][:, :HALF])).astype(BF16)
    for k, v in enumerate([y0[...]] + [r[:, HALF:] for r in parts]):
        h0 = xor(x, k) * 4
        for d in range(2):
            for h in range(4):
                at = (d * 4 + h) * W
                y_ref[d, h0 + h] = v[:, at : at + W]


def last_kernel(own_ref, got_ref, dw1_ref, dw2_ref):
    core = lax.rem(lax.axis_index("space"), 2)
    own, got = own_ref[...], got_ref[...]
    both = [jnp.where(core == 0, own, got), jnp.where(core == 0, got, own)]
    both = jnp.concatenate(both, axis=1) * (1.0 / 256.0)
    for t in range(27):
        dw2_ref[t] = both[:, t * W : (t + 1) * W]
        dw1_ref[t] = both[:, K2 + t * 64 : K2 + (t + 1) * 64]


def local(act_in, w_first, w_second, grad_out):
    X = [[(z * 4 + x, z * 4 + (x ^ k)) for z in range(4) for x in range(4)] for k in range(4)]
    Z = [[(z * 4 + x, (z ^ k) * 4 + x) for z in range(4) for x in range(4)] for k in range(4)]
    up = [(i, (i + 1) % 8) for i in range(8)]
    down = [((i + 1) % 8, i) for i in range(8)]
    other = [(i, i ^ 1) for i in range(8)]
    x = lax.rem(lax.axis_index("filt"), 4)

    (w0,) = run(pack_first_kernel, [sds((8, K1P), BF16)], [jnp.transpose(w_first, (0, 2, 1))])
    joint = ("space", "filt")

    def zed(k0, k1):
        return [(p * 16 + f, p * 16 + (f ^ (4 * (k1 if p % 2 else k0)))) for p in range(8) for f in range(16)]

    p1 = lax.ppermute(w0, joint, zed(1, 2))
    p2 = lax.ppermute(w0, joint, zed(0, 3))

    w_second, grad_out, w0 = lax.optimization_barrier((w_second, grad_out, w0))
    act_in, p1 = lax.optimization_barrier((act_in, p1))
    rows = jnp.pad(jnp.transpose(act_in[0], (1, 2, 0, 3)), ((0, 0), (3, 3), (0, 0), (0, 0)))
    xo = lax.dynamic_slice_in_dim(rows, x * 4, 10, axis=1).reshape(20, 64, W)
    a = run(
        prepare_kernel,
        [sds((8, K1P + 12 * W), BF16)] * 4,
        [jnp.transpose(w_second, (0, 2, 1)), grad_out[0]],
        [pltpu.VMEM((2, 18, 8, W), F32), pltpu.VMEM((8, K2), F32)],
        10**9,
    )
    xp = lax.ppermute(xo, "space", up)
    xn = lax.ppermute(xo, "space", down)

    a, p1, p2 = lax.optimization_barrier((a, p1, p2))
    b = run(pack_kernel, [sds((8, 3 * K1P + 12 * W), BF16)] * 4, [w0, p1, p2] + list(a))
    b = [b[0]] + [lax.ppermute(b[k], "filt", X[k]) for k in (1, 2, 3)]
    half, go = run(
        order_kernel,
        [sds((96, K1P), BF16), sds((32, 12 * W), BF16)],
        b,
        [pltpu.VMEM((96, K1P), F32), pltpu.VMEM((32, 12 * W), F32)],
    )
    half_got = lax.ppermute(half, "space", other)

    (xi,) = run(widen_kernel, [sds((60, 192, W), BF16)], [xo, xp, xn], flops=8 * 10**8)
    slope, xa = run(
        conv_first_kernel,
        [sds((32, 1024), F32), sds((32, 384, W), BF16)],
        [half, half_got, xi],
        [pltpu.VMEM((32, 128, W), F32)],
        4 * 10**9,
    )
    y, gs0, gs1, w2b = run(
        conv_second_kernel,
        [sds((32, 1024), BF16), sds((6, 32, W), BF16), sds((6, 32, W), BF16), sds((128, KB), BF16)],
        [half, half_got, go, xa],
        [pltpu.VMEM((32, K2), F32), pltpu.VMEM((32, K2), BF16)],
    )
    gp = lax.ppermute(gs1, "space", up)
    gn = lax.ppermute(gs0, "space", down)
    (dw2,) = run(second_kernel, [sds((32, K2), F32)], [xa, gs0, gs1], flops=25 * 10**8)

    own, *s = run(
        back_kernel,
        [sds((32, 1024), F32)] + [sds((32, 1024), BF16)] * 3,
        [gs0, gs1, gp, gn, w2b],
        [pltpu.VMEM((24, 96, W), BF16), pltpu.VMEM((128, 1024), F32)],
    )
    s, dw2 = lax.optimization_barrier((s, dw2))
    s = [lax.ppermute(s[k - 1], "filt", Z[k]) for k in (1, 2, 3)]

    keep, give = run(
        first_kernel,
        [sds((32, HALF), F32)] * 2,
        [own] + s + [slope, xi, dw2],
        [pltpu.VMEM((32, 2 * HALF), F32)],
    )
    got = lax.ppermute(give, "space", other)
    o, yo, *s = run(
        chip_kernel,
        [sds((8, HALF), F32), sds((8, 1024), F32)] + [sds((8, HALF + 1024), BF16)] * 3,
        [keep, got, y],
        [pltpu.VMEM((32, HALF), F32), pltpu.VMEM((32, 1024), F32)],
    )
    s = [lax.ppermute(s[k - 1], "filt", X[k]) for k in (1, 2, 3)]
    part, yt = run(sum_kernel, [sds((8, HALF), BF16), sds((2, 16, 8, W), F32)], [o, yo] + s)
    y_out = jnp.transpose(yt, (2, 0, 1, 3)).astype(BF16)[None]

    q = [part] + [lax.ppermute(part, "space", [(i, i ^ (2 * k)) for i in range(8)]) for k in (1, 2, 3)]
    q = [v.astype(F32) for v in q]
    part = ((q[0] + q[1]) + (q[2] + q[3])).astype(BF16)
    part = part.astype(F32) + lax.ppermute(part, "sample", [(0, 1), (1, 0)]).astype(F32)
    got = lax.ppermute(part, "space", other)
    dw1, dw2 = run(last_kernel, [sds((27, 8, 64), F32), sds((27, 8, 128), F32)], [part, got])
    return y_out, jnp.transpose(dw1, (0, 2, 1)), jnp.transpose(dw2, (0, 2, 1))


def solution(mesh):
    placed = (
        P("sample", None, "space", None, None),
        P(None, None, "filt"),
        P(None, None, "filt"),
        P("sample", "filt", "space", None, None),
    )
    return jax.shard_map(
        local,
        mesh=mesh,
        in_specs=placed,
        out_specs=(
            P("sample", "filt", "space", None, None),
            P(None, None, "filt"),
            P(None, None, "filt"),
        ),
        check_vma=False,
    )
```

```python
import jax
import jax.numpy as jnp
from jax import lax
from jax.experimental import pallas as pl
from jax.experimental.pallas import tpu as pltpu
from jax.sharding import PartitionSpec as P

F32 = jnp.float32
BF16 = jnp.bfloat16
W = 128
K1, K2 = 27 * 64, 27 * 128
K1P = 1792
HALF = 2688
KB = 896
VMEM = pl.BlockSpec(memory_space=pltpu.VMEM)
NT = (((1,), (1,)), ((), ()))


def run(kernel, outs, args, scratch=(), flops=10**8):
    return pl.pallas_call(
        kernel,
        out_shape=outs,
        in_specs=[VMEM] * len(args),
        out_specs=[VMEM] * len(outs),
        scratch_shapes=list(scratch),
        cost_estimate=pl.CostEstimate(flops=flops, bytes_accessed=10**5, transcendentals=0),
        compiler_params=pltpu.CompilerParams(vmem_limit_bytes=20 * 1024 * 1024),
    )(*args)


def sds(shape, dtype):
    return jax.ShapeDtypeStruct(shape, dtype)


def split():
    f = lax.axis_index("filt")
    return lax.rem(f, 4), lax.div(f, 4)


def xor(a, k):
    return lax.bitwise_xor(a, jnp.int32(k))


def rows8(i):
    return pl.ds(pl.multiple_of(i * 8, 8), 8)


def rows32(i):
    return pl.ds(pl.multiple_of(i * 32, 32), 32)


def lanes(core):
    return pl.ds(pl.multiple_of(core * HALF, W), HALF)


def shifted(x):
    lane = lax.broadcasted_iota(jnp.int32, x.shape, 1)
    left = jnp.where(lane == 0, 0.0, pltpu.roll(x, 1, 1))
    right = jnp.where(lane == W - 1, 0.0, pltpu.roll(x, W - 1, 1))
    return left, x, right


def height_taps(row):
    zero = jnp.zeros((32, W), BF16)
    taps = []
    for b in range(3):
        cells = []
        for d in range(2):
            cells += [zero] * b + [row(d, h) for h in range(4)] + [zero] * (2 - b)
        taps.append(jnp.concatenate(cells, axis=1))
    return jnp.concatenate(taps, axis=0)


def logistic(v):
    return 0.5 * jnp.tanh(0.5 * v) + 0.5


def pack_first_kernel(w1_ref, out):
    w1 = [w1_ref[t].astype(F32) for t in range(27)]
    out[...] = jnp.concatenate(w1 + [jnp.zeros((8, K1P - K1), F32)], axis=1).astype(BF16)


def prepare_kernel(w2_ref, g_ref, b0, b1, b2, b3, rows_ref, acc):
    x, _ = split()
    core = lax.rem(lax.axis_index("space"), 2)
    for t in range(27):
        acc[:, t * W : (t + 1) * W] = w2_ref[t].astype(F32)
    w2 = acc[:, pl.ds(pl.multiple_of(core * (13 * W), W), K1P)]
    for d in range(2):
        t = jnp.swapaxes(g_ref[:, d].astype(F32), 0, 1)
        rows_ref[d, 0] = jnp.zeros((8, W), F32)
        rows_ref[d, 17] = jnp.zeros((8, W), F32)
        rows_ref[d, 1:17] = t
    for k, out in enumerate((b0, b1, b2, b3)):
        h0 = xor(x, k) * 4
        parts = [rows_ref[d, h0 + h] for d in range(2) for h in range(6)]
        out[...] = jnp.concatenate([w2] + parts, axis=1).astype(BF16)


def pack_kernel(w0_ref, p1_ref, p2_ref, a0, a1, a2, a3, b0, b1, b2, b3):
    _, zl = split()
    core = lax.rem(lax.axis_index("space"), 2)
    w0, p1, p2 = w0_ref[...], p1_ref[...], p2_ref[...]
    same, other = jnp.where(core == 0, w0, p1), jnp.where(core == 0, p1, p2)
    even = lax.rem(zl, 2) == 0
    low, high = jnp.where(even, same, other), jnp.where(even, other, same)
    for a, b in zip((a0, a1, a2, a3), (b0, b1, b2, b3)):
        b[:, :K1P] = low
        b[:, K1P : 2 * K1P] = high
        b[:, 2 * K1P :] = a[...]


def order_kernel(b0, b1, b2, b3, half_ref, go_ref, acc, acc_go):
    x, _ = split()
    for k, b in enumerate((b0, b1, b2, b3)):
        v = b[...].astype(F32)
        for j in range(3):
            acc[rows8(j * 4 + xor(x, k)), :] = v[:, j * K1P : (j + 1) * K1P]
        acc_go[rows8(xor(x, k)), :] = v[:, 3 * K1P :]
    half_ref[...] = acc[...].astype(BF16)
    go_ref[...] = acc_go[...].astype(BF16)


def widen(v, out, r):
    for k, part in enumerate(shifted(v)):
        out[r, k * 64 : (k + 1) * 64] = part.astype(BF16)


def widen_own_kernel(xo_ref, own_ref):
    for r in range(20):
        widen(xo_ref[r].astype(F32), own_ref, r)


def widen_rim_kernel(xp_ref, xn_ref, rim_ref):
    p = lax.axis_index("space")
    for base, ref, inside in ((0, xp_ref, p > 0), (20, xn_ref, p < 7)):
        for r in range(20):
            widen(jnp.where(inside, ref[r].astype(F32), 0.0), rim_ref, base + r)


def input_row(own_ref, rim_ref, layer, height):
    if 2 <= layer <= 3:
        return own_ref[(layer - 2) * 10 + height]
    return rim_ref[(layer if layer < 2 else layer - 2) * 10 + height]


def conv_first_kernel(own_ref, got_ref, xo_ref, xr_ref, slope_ref, xa_ref, zs):
    x, zl = split()
    p = lax.axis_index("space")
    own, got = own_ref[:64], got_ref[:64]
    first = lax.rem(lax.div(zl, 2) + p, 2) == 0
    w1 = jnp.concatenate([jnp.where(first, own, got), jnp.where(first, got, own)], axis=0)[:, :K1]

    for i in range(16):
        dd, hh = i // 4, i % 4 * 2
        cols = []
        for j in range(2):
            cols.append(
                jnp.concatenate(
                    [input_row(xo_ref, xr_ref, dd + a, hh + j + b) for a in range(3) for b in range(3)], axis=0
                )
            )
        z = jnp.dot(w1, jnp.concatenate(cols, axis=1), preferred_element_type=F32)
        depth = p * 2 - 1 + dd
        for j in range(2):
            height = x * 4 - 2 + hh + j
            inside = (depth >= 0) & (depth < 16) & (height >= 0) & (height < 16)
            zr = z[:, j * W : (j + 1) * W]
            r = dd * 8 + hh + j
            zs[r] = zr
            act = jnp.where(inside, zr * logistic(zr), 0.0).astype(BF16).astype(F32)
            left, mid, right = shifted(act)
            xa_ref[r, 0:128] = left.astype(BF16)
            xa_ref[r, 128:256] = mid.astype(BF16)
            xa_ref[r, 256:384] = right.astype(BF16)

    for d in range(2):
        for h in range(4):
            v = zs[(d + 1) * 8 + h + 2, rows32(zl), :]
            q = logistic(v)
            slope_ref[:, (d * 4 + h) * W : (d * 4 + h + 1) * W] = q * (1.0 + v * (1.0 - q))


def conv_second_kernel(own_ref, got_ref, go_ref, xa_ref, y_ref, gs0_ref, gs1_ref, w2b_ref, acc, w2_ref):
    first = lax.rem(lax.axis_index("space"), 2) == 0
    own, got = own_ref[64:], got_ref[64:]
    w2_ref[:, : 14 * W] = jnp.where(first, own, got)
    w2_ref[:, 14 * W :] = jnp.where(first, got, own)[:, W:]
    acc[...] = w2_ref[...].astype(F32)
    for j in range(7):
        taps = [acc[:, t * W : (t + 1) * W] if t < 27 else jnp.zeros((32, W), F32) for t in range(4 * j, 4 * j + 4)]
        w2b_ref[:, j * W : (j + 1) * W] = jnp.concatenate(taps, axis=0).T.astype(BF16)
    planes = [[], []]
    for dd in range(4):
        taps = [a for a in range(3) if 0 <= dd - a <= 1]
        w = jnp.concatenate(
            [w2_ref[:, t * 384 : (t + 1) * 384] for a in taps for t in range(3 * a, 3 * a + 3)], axis=0
        )
        col = jnp.concatenate([xa_ref[dd * 8 + h] for h in range(8)], axis=1)
        part = jnp.dot(w, col, preferred_element_type=F32)
        for k, a in enumerate(taps):
            for b in range(3):
                at = (k * 3 + b) * 32
                planes[dd - a].append(part[at : at + 32, b * W : (b + 6) * W])
    for d in range(2):
        t = planes[d]
        z = ((t[0] + t[1]) + (t[2] + t[3])) + ((t[4] + t[5]) + (t[6] + t[7])) + t[8]
        for hh in range(6):
            v = z[:, hh * W : (hh + 1) * W]
            q = logistic(v)
            if 1 <= hh <= 4:
                at = (d * 4 + hh - 1) * W
                y_ref[:, at : at + W] = (v * q).astype(BF16)
            g = go_ref[:, (d * 6 + hh) * W : (d * 6 + hh + 1) * W].astype(F32)
            gs = (g * (q * (1.0 + v * (1.0 - q)))).astype(BF16)
            (gs0_ref if d == 0 else gs1_ref)[hh] = gs


def second_kernel(xa_ref, gs0_ref, gs1_ref, dw_ref):
    left = height_taps(lambda d, h: (gs0_ref, gs1_ref)[d][h + 1])
    for a in range(3):
        col = jnp.concatenate([xa_ref[(d + a) * 8 + h + 1] for d in range(2) for h in range(6)], axis=1)
        dw = lax.dot_general(left, col, NT, preferred_element_type=F32)
        for b in range(3):
            at = (a * 3 + b) * 384
            dw_ref[:, at : at + 384] = dw[b * 32 : (b + 1) * 32]


def back_kernel(gs0_ref, gs1_ref, gp_ref, gn_ref, w2b_ref, own_ref, s1, s2, s3, g3, acc):
    _, zl = split()
    p = lax.axis_index("space")
    sides = ((gp_ref, p > 0), (gs0_ref, None), (gs1_ref, None), (gn_ref, p < 7))
    for d, (ref, inside) in enumerate(sides):
        for h in range(6):
            v = ref[h].astype(F32)
            before, mid, after = shifted(v if inside is None else jnp.where(inside, v, 0.0))
            g3[d * 6 + h, 0:32] = after.astype(BF16)
            g3[d * 6 + h, 32:64] = mid.astype(BF16)
            g3[d * 6 + h, 64:96] = before.astype(BF16)
    w = w2b_ref[...]
    for d in range(2):
        for hp in range(2):
            cols = []
            for j in range(2):
                h = hp * 2 + j
                cols.append(
                    jnp.concatenate(
                        [g3[(d + 2 - a) * 6 + h + 2 - b] for a in range(3) for b in range(3)]
                        + [jnp.zeros((32, W), BF16)],
                        axis=0,
                    )
                )
            at = (d * 4 + hp * 2) * W
            acc[:, at : at + 2 * W] = jnp.dot(w, jnp.concatenate(cols, axis=1), preferred_element_type=F32)
    own_ref[...] = acc[rows32(zl), :]
    for k, out in enumerate((s1, s2, s3)):
        out[...] = acc[rows32(xor(zl, k + 1)), :].astype(BF16)


def first_kernel(own_ref, r1, r2, r3, slope_ref, xo_ref, xr_ref, dw2_ref, keep_ref, give_ref, acc):
    core = lax.rem(lax.axis_index("space"), 2)
    back = (own_ref[...] + r1[...].astype(F32)) + (r2[...].astype(F32) + r3[...].astype(F32))
    gf = (back * slope_ref[...]).astype(BF16)
    left = height_taps(lambda d, h: gf[:, (d * 4 + h) * W : (d * 4 + h + 1) * W])
    col = jnp.concatenate(
        [
            jnp.concatenate(
                [input_row(xo_ref, xr_ref, d + 1 + a, h + 2) for d in range(2) for h in range(6)], axis=1
            )
            for a in range(3)
        ],
        axis=0,
    )
    dw = lax.dot_general(left, col, NT, preferred_element_type=F32)
    parts = [dw[b * 32 : (b + 1) * 32] for b in range(3)]
    acc[:, :K2] = dw2_ref[...]
    acc[:, K2:] = jnp.concatenate(parts + [jnp.zeros((32, 2 * HALF - K2 - K1), F32)], axis=1)
    keep_ref[...] = acc[:, lanes(core)]
    give_ref[...] = acc[:, lanes(1 - core)]


def chip_kernel(keep_ref, got_ref, y_ref, o0, y0, s1, s2, s3, acc, yacc):
    x, _ = split()
    acc[...] = keep_ref[...] + got_ref[...]
    yacc[...] = y_ref[...].astype(F32)
    o0[...] = acc[rows8(x), :]
    y0[...] = yacc[rows8(x), :]
    for k, out in enumerate((s1, s2, s3)):
        at = rows8(xor(x, k + 1))
        out[...] = jnp.concatenate([acc[at, :], yacc[at, :]], axis=1).astype(BF16)


def sum_kernel(o0, y0, r1, r2, r3, dw_ref, y_ref):
    x, _ = split()
    parts = [r[...].astype(F32) for r in (r1, r2, r3)]
    dw_ref[...] = ((o0[...] + parts[0][:, :HALF]) + (parts[1][:, :HALF] + parts[2][:, :HALF])).astype(BF16)
    for k, v in enumerate([y0[...]] + [r[:, HALF:] for r in parts]):
        h0 = xor(x, k) * 4
        for d in range(2):
            for h in range(4):
                at = (d * 4 + h) * W
                y_ref[d, h0 + h] = v[:, at : at + W]


def last_kernel(own_ref, got_ref, dw1_ref, dw2_ref):
    core = lax.rem(lax.axis_index("space"), 2)
    own, got = own_ref[...], got_ref[...]
    both = [jnp.where(core == 0, own, got), jnp.where(core == 0, got, own)]
    both = jnp.concatenate(both, axis=1) * (1.0 / 256.0)
    for t in range(27):
        a, b, c = t // 9, t // 3 % 3, t % 3
        at = K2 + b * 576 + a * 192 + c * 64
        dw2_ref[t] = both[:, t * W : (t + 1) * W]
        dw1_ref[t] = both[:, at : at + 64]


def local(act_in, w_first, w_second, grad_out):
    X = [[(z * 4 + x, z * 4 + (x ^ k)) for z in range(4) for x in range(4)] for k in range(4)]
    Z = [[(z * 4 + x, (z ^ k) * 4 + x) for z in range(4) for x in range(4)] for k in range(4)]
    up = [(i, (i + 1) % 8) for i in range(8)]
    down = [((i + 1) % 8, i) for i in range(8)]
    other = [(i, i ^ 1) for i in range(8)]
    x = lax.rem(lax.axis_index("filt"), 4)

    (w0,) = run(pack_first_kernel, [sds((8, K1P), BF16)], [jnp.transpose(w_first, (0, 2, 1))])
    joint = ("space", "filt")

    def zed(k0, k1):
        return [(p * 16 + f, p * 16 + (f ^ (4 * (k1 if p % 2 else k0)))) for p in range(8) for f in range(16)]

    p1 = lax.ppermute(w0, joint, zed(1, 2))
    p2 = lax.ppermute(w0, joint, zed(0, 3))

    w_second, grad_out, w0 = lax.optimization_barrier((w_second, grad_out, w0))
    act_in, p1 = lax.optimization_barrier((act_in, p1))
    rows = jnp.pad(jnp.transpose(act_in[0], (1, 2, 0, 3)), ((0, 0), (3, 3), (0, 0), (0, 0)))
    xo = lax.dynamic_slice_in_dim(rows, x * 4, 10, axis=1).reshape(20, 64, W)
    a = run(
        prepare_kernel,
        [sds((8, K1P + 12 * W), BF16)] * 4,
        [jnp.transpose(w_second, (0, 2, 1)), grad_out[0]],
        [pltpu.VMEM((2, 18, 8, W), F32), pltpu.VMEM((8, K2), F32)],
        10**9,
    )
    xp = lax.ppermute(xo, "space", up)
    xn = lax.ppermute(xo, "space", down)

    a, p1, p2 = lax.optimization_barrier((a, p1, p2))
    b = run(pack_kernel, [sds((8, 3 * K1P + 12 * W), BF16)] * 4, [w0, p1, p2] + list(a))
    b = [b[0]] + [lax.ppermute(b[k], "filt", X[k]) for k in (1, 2, 3)]
    half, go = run(
        order_kernel,
        [sds((96, K1P), BF16), sds((32, 12 * W), BF16)],
        b,
        [pltpu.VMEM((96, K1P), F32), pltpu.VMEM((32, 12 * W), F32)],
    )
    half_got = lax.ppermute(half, "space", other)

    (xw,) = run(widen_own_kernel, [sds((20, 192, W), BF16)], [xo], flops=3 * 10**8)
    (xr,) = run(widen_rim_kernel, [sds((40, 192, W), BF16)], [xp, xn], flops=6 * 10**8)
    slope, xa = run(
        conv_first_kernel,
        [sds((32, 1024), F32), sds((32, 384, W), BF16)],
        [half, half_got, xw, xr],
        [pltpu.VMEM((32, 128, W), F32)],
        4 * 10**9,
    )
    y, gs0, gs1, w2b = run(
        conv_second_kernel,
        [sds((32, 1024), BF16), sds((6, 32, W), BF16), sds((6, 32, W), BF16), sds((128, KB), BF16)],
        [half, half_got, go, xa],
        [pltpu.VMEM((32, K2), F32), pltpu.VMEM((32, K2), BF16)],
    )
    gp = lax.ppermute(gs1, "space", up)
    gn = lax.ppermute(gs0, "space", down)
    (dw2,) = run(second_kernel, [sds((32, K2), F32)], [xa, gs0, gs1], flops=25 * 10**8)

    own, *s = run(
        back_kernel,
        [sds((32, 1024), F32)] + [sds((32, 1024), BF16)] * 3,
        [gs0, gs1, gp, gn, w2b],
        [pltpu.VMEM((24, 96, W), BF16), pltpu.VMEM((128, 1024), F32)],
    )
    s, dw2 = lax.optimization_barrier((s, dw2))
    s = [lax.ppermute(s[k - 1], "filt", Z[k]) for k in (1, 2, 3)]

    keep, give = run(
        first_kernel,
        [sds((32, HALF), F32)] * 2,
        [own] + s + [slope, xw, xr, dw2],
        [pltpu.VMEM((32, 2 * HALF), F32)],
    )
    got = lax.ppermute(give, "space", other)
    o, yo, *s = run(
        chip_kernel,
        [sds((8, HALF), F32), sds((8, 1024), F32)] + [sds((8, HALF + 1024), BF16)] * 3,
        [keep, got, y],
        [pltpu.VMEM((32, HALF), F32), pltpu.VMEM((32, 1024), F32)],
    )
    s = [lax.ppermute(s[k - 1], "filt", X[k]) for k in (1, 2, 3)]
    part, yt = run(sum_kernel, [sds((8, HALF), BF16), sds((2, 16, 8, W), F32)], [o, yo] + s)
    y_out = jnp.transpose(yt, (2, 0, 1, 3)).astype(BF16)[None]

    q = [part] + [lax.ppermute(part, "space", [(i, i ^ (2 * k)) for i in range(8)]) for k in (1, 2, 3)]
    q = [v.astype(F32) for v in q]
    part = ((q[0] + q[1]) + (q[2] + q[3])).astype(BF16)
    part = part.astype(F32) + lax.ppermute(part, "sample", [(0, 1), (1, 0)]).astype(F32)
    got = lax.ppermute(part, "space", other)
    dw1, dw2 = run(last_kernel, [sds((27, 8, 64), F32), sds((27, 8, 128), F32)], [part, got])
    return y_out, jnp.transpose(dw1, (0, 2, 1)), jnp.transpose(dw2, (0, 2, 1))


def solution(mesh):
    placed = (
        P("sample", None, "space", None, None),
        P(None, None, "filt"),
        P(None, None, "filt"),
        P("sample", "filt", "space", None, None),
    )
    return jax.shard_map(
        local,
        mesh=mesh,
        in_specs=placed,
        out_specs=(
            P("sample", "filt", "space", None, None),
            P(None, None, "filt"),
            P(None, None, "filt"),
        ),
        check_vma=False,
    )
```

```python
import jax
import jax.numpy as jnp
from jax import lax
from jax.experimental import pallas as pl
from jax.experimental.pallas import tpu as pltpu
from jax.sharding import PartitionSpec as P

F32 = jnp.float32
BF16 = jnp.bfloat16
W = 128
K1, K2 = 27 * 64, 27 * 128
K1P = 1792
HALF = 2688
KB = 896
VMEM = pl.BlockSpec(memory_space=pltpu.VMEM)
NT = (((1,), (1,)), ((), ()))


def run(kernel, outs, args, scratch=(), flops=10**8):
    return pl.pallas_call(
        kernel,
        out_shape=outs,
        in_specs=[VMEM] * len(args),
        out_specs=[VMEM] * len(outs),
        scratch_shapes=list(scratch),
        cost_estimate=pl.CostEstimate(flops=flops, bytes_accessed=10**5, transcendentals=0),
        compiler_params=pltpu.CompilerParams(vmem_limit_bytes=20 * 1024 * 1024),
    )(*args)


def sds(shape, dtype):
    return jax.ShapeDtypeStruct(shape, dtype)


def split():
    f = lax.axis_index("filt")
    return lax.rem(f, 4), lax.div(f, 4)


def xor(a, k):
    return lax.bitwise_xor(a, jnp.int32(k))


def rows8(i):
    return pl.ds(pl.multiple_of(i * 8, 8), 8)


def rows32(i):
    return pl.ds(pl.multiple_of(i * 32, 32), 32)


def lanes(core):
    return pl.ds(pl.multiple_of(core * HALF, W), HALF)


def shifted(x):
    lane = lax.broadcasted_iota(jnp.int32, x.shape, 1)
    left = jnp.where(lane == 0, 0.0, pltpu.roll(x, 1, 1))
    right = jnp.where(lane == W - 1, 0.0, pltpu.roll(x, W - 1, 1))
    return left, x, right


def height_taps(row):
    zero = jnp.zeros((32, W), BF16)
    taps = []
    for b in range(3):
        cells = []
        for d in range(2):
            cells += [zero] * b + [row(d, h) for h in range(4)] + [zero] * (2 - b)
        taps.append(jnp.concatenate(cells, axis=1))
    return jnp.concatenate(taps, axis=0)


def logistic(v):
    return 0.5 * jnp.tanh(0.5 * v) + 0.5


def pack_first_kernel(w1_ref, out):
    w1 = [w1_ref[t].astype(F32) for t in range(27)]
    out[...] = jnp.concatenate(w1 + [jnp.zeros((8, K1P - K1), F32)], axis=1).astype(BF16)


def prepare_kernel(w2_ref, g_ref, b0, b1, b2, b3, rows_ref, acc):
    x, _ = split()
    core = lax.rem(lax.axis_index("space"), 2)
    for t in range(27):
        acc[:, t * W : (t + 1) * W] = w2_ref[t].astype(F32)
    w2 = acc[:, pl.ds(pl.multiple_of(core * (13 * W), W), K1P)]
    for d in range(2):
        t = jnp.swapaxes(g_ref[:, d].astype(F32), 0, 1)
        rows_ref[d, 0] = jnp.zeros((8, W), F32)
        rows_ref[d, 17] = jnp.zeros((8, W), F32)
        rows_ref[d, 1:17] = t
    for k, out in enumerate((b0, b1, b2, b3)):
        h0 = xor(x, k) * 4
        parts = [rows_ref[d, h0 + h] for d in range(2) for h in range(6)]
        out[...] = jnp.concatenate([w2] + parts, axis=1).astype(BF16)


def pack_kernel(w0_ref, p1_ref, p2_ref, a0, a1, a2, a3, b0, b1, b2, b3):
    _, zl = split()
    core = lax.rem(lax.axis_index("space"), 2)
    w0, p1, p2 = w0_ref[...], p1_ref[...], p2_ref[...]
    same, other = jnp.where(core == 0, w0, p1), jnp.where(core == 0, p1, p2)
    even = lax.rem(zl, 2) == 0
    low, high = jnp.where(even, same, other), jnp.where(even, other, same)
    for a, b in zip((a0, a1, a2, a3), (b0, b1, b2, b3)):
        b[:, :K1P] = low
        b[:, K1P : 2 * K1P] = high
        b[:, 2 * K1P :] = a[...]


def order_kernel(b0, b1, b2, b3, half_ref, go_ref, acc, acc_go):
    x, _ = split()
    for k, b in enumerate((b0, b1, b2, b3)):
        v = b[...].astype(F32)
        for j in range(3):
            acc[rows8(j * 4 + xor(x, k)), :] = v[:, j * K1P : (j + 1) * K1P]
        acc_go[rows8(xor(x, k)), :] = v[:, 3 * K1P :]
    half_ref[...] = acc[...].astype(BF16)
    go_ref[...] = acc_go[...].astype(BF16)


def widen(v, out, r):
    for k, part in enumerate(shifted(v)):
        out[r, k * 64 : (k + 1) * 64] = part.astype(BF16)


def widen_own_kernel(xo_ref, own_ref):
    for r in range(20):
        widen(xo_ref[r].astype(F32), own_ref, r)


def widen_rim_kernel(chip_ref, next_ref, rim_ref):
    p = lax.axis_index("space")
    first = lax.rem(p, 2) == 0
    for r in range(20):
        chip, far = chip_ref[r].astype(F32), next_ref[r].astype(F32)
        widen(jnp.where(p > 0, jnp.where(first, far, chip), 0.0), rim_ref, r)
        widen(jnp.where(p < 7, jnp.where(first, chip, far), 0.0), rim_ref, 20 + r)


def input_row(own_ref, rim_ref, layer, height):
    if 2 <= layer <= 3:
        return own_ref[(layer - 2) * 10 + height]
    return rim_ref[(layer if layer < 2 else layer - 2) * 10 + height]


def conv_first_kernel(own_ref, got_ref, xo_ref, xr_ref, slope_ref, xa_ref, zs):
    x, zl = split()
    p = lax.axis_index("space")
    own, got = own_ref[:64], got_ref[:64]
    first = lax.rem(lax.div(zl, 2) + p, 2) == 0
    w1 = jnp.concatenate([jnp.where(first, own, got), jnp.where(first, got, own)], axis=0)[:, :K1]

    for i in range(16):
        dd, hh = i // 4, i % 4 * 2
        cols = []
        for j in range(2):
            cols.append(
                jnp.concatenate(
                    [input_row(xo_ref, xr_ref, dd + a, hh + j + b) for a in range(3) for b in range(3)], axis=0
                )
            )
        z = jnp.dot(w1, jnp.concatenate(cols, axis=1), preferred_element_type=F32)
        depth = p * 2 - 1 + dd
        for j in range(2):
            height = x * 4 - 2 + hh + j
            inside = (depth >= 0) & (depth < 16) & (height >= 0) & (height < 16)
            zr = z[:, j * W : (j + 1) * W]
            r = dd * 8 + hh + j
            zs[r] = zr
            act = jnp.where(inside, zr * logistic(zr), 0.0).astype(BF16).astype(F32)
            left, mid, right = shifted(act)
            xa_ref[r, 0:128] = left.astype(BF16)
            xa_ref[r, 128:256] = mid.astype(BF16)
            xa_ref[r, 256:384] = right.astype(BF16)

    for d in range(2):
        for h in range(4):
            v = zs[(d + 1) * 8 + h + 2, rows32(zl), :]
            q = logistic(v)
            slope_ref[:, (d * 4 + h) * W : (d * 4 + h + 1) * W] = q * (1.0 + v * (1.0 - q))


def conv_second_kernel(
    own_ref, got_ref, go_ref, xa_ref, y_ref, gs0_ref, gs1_ref, chip_ref, next_ref, w2b_ref, acc, w2_ref
):
    first = lax.rem(lax.axis_index("space"), 2) == 0
    own, got = own_ref[64:], got_ref[64:]
    w2_ref[:, : 14 * W] = jnp.where(first, own, got)
    w2_ref[:, 14 * W :] = jnp.where(first, got, own)[:, W:]
    acc[...] = w2_ref[...].astype(F32)
    for j in range(7):
        taps = [acc[:, t * W : (t + 1) * W] if t < 27 else jnp.zeros((32, W), F32) for t in range(4 * j, 4 * j + 4)]
        w2b_ref[:, j * W : (j + 1) * W] = jnp.concatenate(taps, axis=0).T.astype(BF16)
    planes = [[], []]
    for dd in range(4):
        taps = [a for a in range(3) if 0 <= dd - a <= 1]
        w = jnp.concatenate(
            [w2_ref[:, t * 384 : (t + 1) * 384] for a in taps for t in range(3 * a, 3 * a + 3)], axis=0
        )
        col = jnp.concatenate([xa_ref[dd * 8 + h] for h in range(8)], axis=1)
        part = jnp.dot(w, col, preferred_element_type=F32)
        for k, a in enumerate(taps):
            for b in range(3):
                at = (k * 3 + b) * 32
                planes[dd - a].append(part[at : at + 32, b * W : (b + 6) * W])
    for d in range(2):
        t = planes[d]
        z = ((t[0] + t[1]) + (t[2] + t[3])) + ((t[4] + t[5]) + (t[6] + t[7])) + t[8]
        for hh in range(6):
            v = z[:, hh * W : (hh + 1) * W]
            q = logistic(v)
            if 1 <= hh <= 4:
                at = (d * 4 + hh - 1) * W
                y_ref[:, at : at + W] = (v * q).astype(BF16)
            g = go_ref[:, (d * 6 + hh) * W : (d * 6 + hh + 1) * W].astype(F32)
            gs = (g * (q * (1.0 + v * (1.0 - q)))).astype(BF16)
            (gs0_ref if d == 0 else gs1_ref)[hh] = gs
    for hh in range(6):
        chip_ref[hh] = jnp.where(first, gs1_ref[hh], gs0_ref[hh])
        next_ref[hh] = jnp.where(first, gs0_ref[hh], gs1_ref[hh])


def second_kernel(xa_ref, gs0_ref, gs1_ref, dw_ref):
    left = height_taps(lambda d, h: (gs0_ref, gs1_ref)[d][h + 1])
    for a in range(3):
        col = jnp.concatenate([xa_ref[(d + a) * 8 + h + 1] for d in range(2) for h in range(6)], axis=1)
        dw = lax.dot_general(left, col, NT, preferred_element_type=F32)
        for b in range(3):
            at = (a * 3 + b) * 384
            dw_ref[:, at : at + 384] = dw[b * 32 : (b + 1) * 32]


def back_kernel(gs0_ref, gs1_ref, chip_ref, next_ref, w2b_ref, own_ref, s1, s2, s3, g3, acc):
    _, zl = split()
    p = lax.axis_index("space")
    first = lax.rem(p, 2) == 0
    for d in range(4):
        for h in range(6):
            if d == 0:
                v = jnp.where(first, next_ref[h].astype(F32), chip_ref[h].astype(F32))
                v = jnp.where(p > 0, v, 0.0)
            elif d == 3:
                v = jnp.where(first, chip_ref[h].astype(F32), next_ref[h].astype(F32))
                v = jnp.where(p < 7, v, 0.0)
            else:
                v = (gs0_ref, gs1_ref)[d - 1][h].astype(F32)
            before, mid, after = shifted(v)
            g3[d * 6 + h, 0:32] = after.astype(BF16)
            g3[d * 6 + h, 32:64] = mid.astype(BF16)
            g3[d * 6 + h, 64:96] = before.astype(BF16)
    w = w2b_ref[...]
    for d in range(2):
        for hp in range(2):
            cols = []
            for j in range(2):
                h = hp * 2 + j
                cols.append(
                    jnp.concatenate(
                        [g3[(d + 2 - a) * 6 + h + 2 - b] for a in range(3) for b in range(3)]
                        + [jnp.zeros((32, W), BF16)],
                        axis=0,
                    )
                )
            at = (d * 4 + hp * 2) * W
            acc[:, at : at + 2 * W] = jnp.dot(w, jnp.concatenate(cols, axis=1), preferred_element_type=F32)
    own_ref[...] = acc[rows32(zl), :]
    for k, out in enumerate((s1, s2, s3)):
        out[...] = acc[rows32(xor(zl, k + 1)), :].astype(BF16)


def first_kernel(own_ref, r1, r2, r3, slope_ref, xo_ref, xr_ref, dw2_ref, keep_ref, give_ref, acc):
    core = lax.rem(lax.axis_index("space"), 2)
    back = (own_ref[...] + r1[...].astype(F32)) + (r2[...].astype(F32) + r3[...].astype(F32))
    gf = (back * slope_ref[...]).astype(BF16)
    left = height_taps(lambda d, h: gf[:, (d * 4 + h) * W : (d * 4 + h + 1) * W])
    col = jnp.concatenate(
        [
            jnp.concatenate(
                [input_row(xo_ref, xr_ref, d + 1 + a, h + 2) for d in range(2) for h in range(6)], axis=1
            )
            for a in range(3)
        ],
        axis=0,
    )
    dw = lax.dot_general(left, col, NT, preferred_element_type=F32)
    parts = [dw[b * 32 : (b + 1) * 32] for b in range(3)]
    acc[:, :K2] = dw2_ref[...]
    acc[:, K2:] = jnp.concatenate(parts + [jnp.zeros((32, 2 * HALF - K2 - K1), F32)], axis=1)
    keep_ref[...] = acc[:, lanes(core)]
    give_ref[...] = acc[:, lanes(1 - core)]


def chip_kernel(keep_ref, got_ref, y_ref, o0, y0, s1, s2, s3, acc, yacc):
    x, _ = split()
    acc[...] = keep_ref[...] + got_ref[...]
    yacc[...] = y_ref[...].astype(F32)
    o0[...] = acc[rows8(x), :]
    y0[...] = yacc[rows8(x), :]
    for k, out in enumerate((s1, s2, s3)):
        at = rows8(xor(x, k + 1))
        out[...] = jnp.concatenate([acc[at, :], yacc[at, :]], axis=1).astype(BF16)


def sum_kernel(o0, y0, r1, r2, r3, dw_ref, y_ref):
    x, _ = split()
    parts = [r[...].astype(F32) for r in (r1, r2, r3)]
    dw_ref[...] = ((o0[...] + parts[0][:, :HALF]) + (parts[1][:, :HALF] + parts[2][:, :HALF])).astype(BF16)
    for k, v in enumerate([y0[...]] + [r[:, HALF:] for r in parts]):
        h0 = xor(x, k) * 4
        for d in range(2):
            for h in range(4):
                at = (d * 4 + h) * W
                y_ref[d, h0 + h] = v[:, at : at + W]


def last_kernel(own_ref, got_ref, dw1_ref, dw2_ref):
    core = lax.rem(lax.axis_index("space"), 2)
    own, got = own_ref[...], got_ref[...]
    both = [jnp.where(core == 0, own, got), jnp.where(core == 0, got, own)]
    both = jnp.concatenate(both, axis=1) * (1.0 / 256.0)
    for t in range(27):
        a, b, c = t // 9, t // 3 % 3, t % 3
        at = K2 + b * 576 + a * 192 + c * 64
        dw2_ref[t] = both[:, t * W : (t + 1) * W]
        dw1_ref[t] = both[:, at : at + 64]


def local(act_in, w_first, w_second, grad_out):
    X = [[(z * 4 + x, z * 4 + (x ^ k)) for z in range(4) for x in range(4)] for k in range(4)]
    Z = [[(z * 4 + x, (z ^ k) * 4 + x) for z in range(4) for x in range(4)] for k in range(4)]
    across = [(i, (i + 1) % 8 if i % 2 else (i + 7) % 8) for i in range(8)]
    other = [(i, i ^ 1) for i in range(8)]
    x = lax.rem(lax.axis_index("filt"), 4)

    (w0,) = run(pack_first_kernel, [sds((8, K1P), BF16)], [jnp.transpose(w_first, (0, 2, 1))])
    joint = ("space", "filt")

    def zed(k0, k1):
        return [(p * 16 + f, p * 16 + (f ^ (4 * (k1 if p % 2 else k0)))) for p in range(8) for f in range(16)]

    p1 = lax.ppermute(w0, joint, zed(1, 2))
    p2 = lax.ppermute(w0, joint, zed(0, 3))

    w_second, grad_out, w0 = lax.optimization_barrier((w_second, grad_out, w0))
    act_in, p1 = lax.optimization_barrier((act_in, p1))
    rows = jnp.pad(jnp.transpose(act_in[0], (1, 2, 0, 3)), ((0, 0), (3, 3), (0, 0), (0, 0)))
    xo = lax.dynamic_slice_in_dim(rows, x * 4, 10, axis=1).reshape(20, 64, W)
    a = run(
        prepare_kernel,
        [sds((8, K1P + 12 * W), BF16)] * 4,
        [jnp.transpose(w_second, (0, 2, 1)), grad_out[0]],
        [pltpu.VMEM((2, 18, 8, W), F32), pltpu.VMEM((8, K2), F32)],
        10**9,
    )
    xchip = lax.ppermute(xo, "space", other)
    xnext = lax.ppermute(xo, "space", across)

    a, p1, p2 = lax.optimization_barrier((a, p1, p2))
    b = run(pack_kernel, [sds((8, 3 * K1P + 12 * W), BF16)] * 4, [w0, p1, p2] + list(a))
    b = [b[0]] + [lax.ppermute(b[k], "filt", X[k]) for k in (1, 2, 3)]
    half, go = run(
        order_kernel,
        [sds((96, K1P), BF16), sds((32, 12 * W), BF16)],
        b,
        [pltpu.VMEM((96, K1P), F32), pltpu.VMEM((32, 12 * W), F32)],
    )
    half_got = lax.ppermute(half, "space", other)

    (xw,) = run(widen_own_kernel, [sds((20, 192, W), BF16)], [xo], flops=3 * 10**8)
    (xr,) = run(widen_rim_kernel, [sds((40, 192, W), BF16)], [xchip, xnext], flops=6 * 10**8)
    slope, xa = run(
        conv_first_kernel,
        [sds((32, 1024), F32), sds((32, 384, W), BF16)],
        [half, half_got, xw, xr],
        [pltpu.VMEM((32, 128, W), F32)],
        4 * 10**9,
    )
    y, gs0, gs1, gchip, gnext, w2b = run(
        conv_second_kernel,
        [sds((32, 1024), BF16)] + [sds((6, 32, W), BF16)] * 4 + [sds((128, KB), BF16)],
        [half, half_got, go, xa],
        [pltpu.VMEM((32, K2), F32), pltpu.VMEM((32, K2), BF16)],
    )
    gchip = lax.ppermute(gchip, "space", other)
    gnext = lax.ppermute(gnext, "space", across)
    (dw2,) = run(second_kernel, [sds((32, K2), F32)], [xa, gs0, gs1], flops=25 * 10**8)

    own, *s = run(
        back_kernel,
        [sds((32, 1024), F32)] + [sds((32, 1024), BF16)] * 3,
        [gs0, gs1, gchip, gnext, w2b],
        [pltpu.VMEM((24, 96, W), BF16), pltpu.VMEM((128, 1024), F32)],
    )
    s, dw2 = lax.optimization_barrier((s, dw2))
    s = [lax.ppermute(s[k - 1], "filt", Z[k]) for k in (1, 2, 3)]

    keep, give = run(
        first_kernel,
        [sds((32, HALF), F32)] * 2,
        [own] + s + [slope, xw, xr, dw2],
        [pltpu.VMEM((32, 2 * HALF), F32)],
    )
    got = lax.ppermute(give, "space", other)
    o, yo, *s = run(
        chip_kernel,
        [sds((8, HALF), F32), sds((8, 1024), F32)] + [sds((8, HALF + 1024), BF16)] * 3,
        [keep, got, y],
        [pltpu.VMEM((32, HALF), F32), pltpu.VMEM((32, 1024), F32)],
    )
    s = [lax.ppermute(s[k - 1], "filt", X[k]) for k in (1, 2, 3)]
    part, yt = run(sum_kernel, [sds((8, HALF), BF16), sds((2, 16, 8, W), F32)], [o, yo] + s)
    y_out = jnp.transpose(yt, (2, 0, 1, 3)).astype(BF16)[None]

    q = [part] + [lax.ppermute(part, "space", [(i, i ^ (2 * k)) for i in range(8)]) for k in (1, 2, 3)]
    q = [v.astype(F32) for v in q]
    part = ((q[0] + q[1]) + (q[2] + q[3])).astype(BF16)
    part = part.astype(F32) + lax.ppermute(part, "sample", [(0, 1), (1, 0)]).astype(F32)
    got = lax.ppermute(part, "space", other)
    dw1, dw2 = run(last_kernel, [sds((27, 8, 64), F32), sds((27, 8, 128), F32)], [part, got])
    return y_out, jnp.transpose(dw1, (0, 2, 1)), jnp.transpose(dw2, (0, 2, 1))


def solution(mesh):
    placed = (
        P("sample", None, "space", None, None),
        P(None, None, "filt"),
        P(None, None, "filt"),
        P("sample", "filt", "space", None, None),
    )
    return jax.shard_map(
        local,
        mesh=mesh,
        in_specs=placed,
        out_specs=(
            P("sample", "filt", "space", None, None),
            P(None, None, "filt"),
            P(None, None, "filt"),
        ),
        check_vma=False,
    )
```

```python
import jax
import jax.numpy as jnp
from jax import lax
from jax.experimental import pallas as pl
from jax.experimental.pallas import tpu as pltpu
from jax.sharding import PartitionSpec as P

F32 = jnp.float32
BF16 = jnp.bfloat16
W = 128
K1, K2 = 27 * 64, 27 * 128
K1P = 1792
HALF = 2688
KB = 896
VMEM = pl.BlockSpec(memory_space=pltpu.VMEM)
NT = (((1,), (1,)), ((), ()))


def run(kernel, outs, args, scratch=(), flops=10**8):
    return pl.pallas_call(
        kernel,
        out_shape=outs,
        in_specs=[VMEM] * len(args),
        out_specs=[VMEM] * len(outs),
        scratch_shapes=list(scratch),
        cost_estimate=pl.CostEstimate(flops=flops, bytes_accessed=10**5, transcendentals=0),
        compiler_params=pltpu.CompilerParams(vmem_limit_bytes=20 * 1024 * 1024),
    )(*args)


def sds(shape, dtype):
    return jax.ShapeDtypeStruct(shape, dtype)


def split():
    f = lax.axis_index("filt")
    return lax.rem(f, 4), lax.div(f, 4)


def xor(a, k):
    return lax.bitwise_xor(a, jnp.int32(k))


def rows8(i):
    return pl.ds(pl.multiple_of(i * 8, 8), 8)


def rows32(i):
    return pl.ds(pl.multiple_of(i * 32, 32), 32)


def lanes(core):
    return pl.ds(pl.multiple_of(core * HALF, W), HALF)


def shifted(x):
    lane = lax.broadcasted_iota(jnp.int32, x.shape, 1)
    left = jnp.where(lane == 0, 0.0, pltpu.roll(x, 1, 1))
    right = jnp.where(lane == W - 1, 0.0, pltpu.roll(x, W - 1, 1))
    return left, x, right


def height_taps(row):
    zero = jnp.zeros((32, W), BF16)
    taps = []
    for b in range(3):
        cells = []
        for d in range(2):
            cells += [zero] * b + [row(d, h) for h in range(4)] + [zero] * (2 - b)
        taps.append(jnp.concatenate(cells, axis=1))
    return jnp.concatenate(taps, axis=0)


def logistic(v):
    return 0.5 * jnp.tanh(0.5 * v) + 0.5


def pack_first_kernel(w1_ref, out):
    w1 = [w1_ref[t].astype(F32) for t in range(27)]
    out[...] = jnp.concatenate(w1 + [jnp.zeros((8, K1P - K1), F32)], axis=1).astype(BF16)


def prepare_kernel(w2_ref, g_ref, b0, b1, b2, b3, rows_ref, acc):
    x, _ = split()
    core = lax.rem(lax.axis_index("space"), 2)
    for t in range(27):
        acc[:, t * W : (t + 1) * W] = w2_ref[t].astype(F32)
    w2 = acc[:, pl.ds(pl.multiple_of(core * (13 * W), W), K1P)]
    for d in range(2):
        t = jnp.swapaxes(g_ref[:, d].astype(F32), 0, 1)
        rows_ref[d, 0] = jnp.zeros((8, W), F32)
        rows_ref[d, 17] = jnp.zeros((8, W), F32)
        rows_ref[d, 1:17] = t
    for k, out in enumerate((b0, b1, b2, b3)):
        h0 = xor(x, k) * 4
        parts = [rows_ref[d, h0 + h] for d in range(2) for h in range(6)]
        out[...] = jnp.concatenate([w2] + parts, axis=1).astype(BF16)


def pack_kernel(w0_ref, p1_ref, p2_ref, a0, a1, a2, a3, b0, b1, b2, b3):
    _, zl = split()
    core = lax.rem(lax.axis_index("space"), 2)
    w0, p1, p2 = w0_ref[...], p1_ref[...], p2_ref[...]
    same, other = jnp.where(core == 0, w0, p1), jnp.where(core == 0, p1, p2)
    even = lax.rem(zl, 2) == 0
    low, high = jnp.where(even, same, other), jnp.where(even, other, same)
    for a, b in zip((a0, a1, a2, a3), (b0, b1, b2, b3)):
        b[:, :K1P] = low
        b[:, K1P : 2 * K1P] = high
        b[:, 2 * K1P :] = a[...]


def order_kernel(b0, b1, b2, b3, half_ref, go_ref, acc, acc_go):
    x, _ = split()
    for k, b in enumerate((b0, b1, b2, b3)):
        v = b[...].astype(F32)
        for j in range(3):
            acc[rows8(j * 4 + xor(x, k)), :] = v[:, j * K1P : (j + 1) * K1P]
        acc_go[rows8(xor(x, k)), :] = v[:, 3 * K1P :]
    half_ref[...] = acc[...].astype(BF16)
    go_ref[...] = acc_go[...].astype(BF16)


def widen(v, out, r):
    for k, part in enumerate(shifted(v)):
        out[r, k * 64 : (k + 1) * 64] = part.astype(BF16)


def widen_own_kernel(xo_ref, own_ref):
    for r in range(20):
        widen(xo_ref[r].astype(F32), own_ref, r)


def widen_rim_kernel(chip_ref, next_ref, rim_ref):
    p = lax.axis_index("space")
    first = lax.rem(p, 2) == 0
    for r in range(20):
        chip, far = chip_ref[r].astype(F32), next_ref[r].astype(F32)
        widen(jnp.where(p > 0, jnp.where(first, far, chip), 0.0), rim_ref, r)
        widen(jnp.where(p < 7, jnp.where(first, chip, far), 0.0), rim_ref, 20 + r)


def input_row(own_ref, rim_ref, layer, height):
    if 2 <= layer <= 3:
        return own_ref[(layer - 2) * 10 + height]
    return rim_ref[(layer if layer < 2 else layer - 2) * 10 + height]


def conv_first_kernel(own_ref, got_ref, xo_ref, xr_ref, slope_ref, xa_ref, zs):
    x, zl = split()
    p = lax.axis_index("space")
    own, got = own_ref[:64], got_ref[:64]
    first = lax.rem(lax.div(zl, 2) + p, 2) == 0
    w1 = jnp.concatenate([jnp.where(first, own, got), jnp.where(first, got, own)], axis=0)[:, :K1]

    for i in range(16):
        dd, hh = i // 4, i % 4 * 2
        cols = []
        for j in range(2):
            cols.append(
                jnp.concatenate(
                    [input_row(xo_ref, xr_ref, dd + a, hh + j + b) for a in range(3) for b in range(3)], axis=0
                )
            )
        z = jnp.dot(w1, jnp.concatenate(cols, axis=1), preferred_element_type=F32)
        depth = p * 2 - 1 + dd
        for j in range(2):
            height = x * 4 - 2 + hh + j
            inside = (depth >= 0) & (depth < 16) & (height >= 0) & (height < 16)
            zr = z[:, j * W : (j + 1) * W]
            r = dd * 8 + hh + j
            zs[r] = zr
            act = jnp.where(inside, zr * logistic(zr), 0.0).astype(BF16).astype(F32)
            left, mid, right = shifted(act)
            xa_ref[r, 0:128] = left.astype(BF16)
            xa_ref[r, 128:256] = mid.astype(BF16)
            xa_ref[r, 256:384] = right.astype(BF16)

    for d in range(2):
        for h in range(4):
            v = zs[(d + 1) * 8 + h + 2, rows32(zl), :]
            q = logistic(v)
            slope_ref[:, (d * 4 + h) * W : (d * 4 + h + 1) * W] = q * (1.0 + v * (1.0 - q))


def conv_second_kernel(
    own_ref, got_ref, go_ref, xa_ref, y_ref, gs0_ref, gs1_ref, chip_ref, next_ref, w2b_ref, acc, w2_ref
):
    first = lax.rem(lax.axis_index("space"), 2) == 0
    own, got = own_ref[64:], got_ref[64:]
    w2_ref[:, : 14 * W] = jnp.where(first, own, got)
    w2_ref[:, 14 * W :] = jnp.where(first, got, own)[:, W:]
    acc[...] = w2_ref[...].astype(F32)
    for j in range(7):
        taps = [acc[:, t * W : (t + 1) * W] if t < 27 else jnp.zeros((32, W), F32) for t in range(4 * j, 4 * j + 4)]
        w2b_ref[:, j * W : (j + 1) * W] = jnp.concatenate(taps, axis=0).T.astype(BF16)
    planes = [[], []]
    for dd in range(4):
        taps = [a for a in range(3) if 0 <= dd - a <= 1]
        w = jnp.concatenate(
            [w2_ref[:, t * 384 : (t + 1) * 384] for a in taps for t in range(3 * a, 3 * a + 3)], axis=0
        )
        col = jnp.concatenate([xa_ref[dd * 8 + h] for h in range(8)], axis=1)
        part = jnp.dot(w, col, preferred_element_type=F32)
        for k, a in enumerate(taps):
            for b in range(3):
                at = (k * 3 + b) * 32
                planes[dd - a].append(part[at : at + 32, b * W : (b + 6) * W])
    for d in range(2):
        t = planes[d]
        z = ((t[0] + t[1]) + (t[2] + t[3])) + ((t[4] + t[5]) + (t[6] + t[7])) + t[8]
        for hh in range(6):
            v = z[:, hh * W : (hh + 1) * W]
            q = logistic(v)
            if 1 <= hh <= 4:
                at = (d * 4 + hh - 1) * W
                y_ref[:, at : at + W] = (v * q).astype(BF16)
            g = go_ref[:, (d * 6 + hh) * W : (d * 6 + hh + 1) * W].astype(F32)
            gs = (g * (q * (1.0 + v * (1.0 - q)))).astype(BF16)
            (gs0_ref if d == 0 else gs1_ref)[hh] = gs
    for hh in range(6):
        chip_ref[hh] = jnp.where(first, gs1_ref[hh], gs0_ref[hh])
        next_ref[hh] = jnp.where(first, gs0_ref[hh], gs1_ref[hh])


def second_kernel(xa_ref, gs0_ref, gs1_ref, dw_ref):
    left = height_taps(lambda d, h: (gs0_ref, gs1_ref)[d][h + 1])
    for a in range(3):
        col = jnp.concatenate([xa_ref[(d + a) * 8 + h + 1] for d in range(2) for h in range(6)], axis=1)
        dw = lax.dot_general(left, col, NT, preferred_element_type=F32)
        for b in range(3):
            at = (a * 3 + b) * 384
            dw_ref[:, at : at + 384] = dw[b * 32 : (b + 1) * 32]


def back_kernel(gs0_ref, gs1_ref, chip_ref, next_ref, w2b_ref, own_ref, s1, s2, s3, g3, acc):
    _, zl = split()
    p = lax.axis_index("space")
    first = lax.rem(p, 2) == 0
    for d in range(4):
        for h in range(6):
            if d == 0:
                v = jnp.where(first, next_ref[h].astype(F32), chip_ref[h].astype(F32))
                v = jnp.where(p > 0, v, 0.0)
            elif d == 3:
                v = jnp.where(first, chip_ref[h].astype(F32), next_ref[h].astype(F32))
                v = jnp.where(p < 7, v, 0.0)
            else:
                v = (gs0_ref, gs1_ref)[d - 1][h].astype(F32)
            before, mid, after = shifted(v)
            g3[d * 6 + h, 0:32] = after.astype(BF16)
            g3[d * 6 + h, 32:64] = mid.astype(BF16)
            g3[d * 6 + h, 64:96] = before.astype(BF16)
    w = w2b_ref[...]
    for d in range(2):
        for hp in range(2):
            cols = []
            for j in range(2):
                h = hp * 2 + j
                cols.append(
                    jnp.concatenate(
                        [g3[(d + 2 - a) * 6 + h + 2 - b] for a in range(3) for b in range(3)]
                        + [jnp.zeros((32, W), BF16)],
                        axis=0,
                    )
                )
            at = (d * 4 + hp * 2) * W
            acc[:, at : at + 2 * W] = jnp.dot(w, jnp.concatenate(cols, axis=1), preferred_element_type=F32)
    own_ref[...] = acc[rows32(zl), :]
    for k, out in enumerate((s1, s2, s3)):
        out[...] = acc[rows32(xor(zl, k + 1)), :].astype(BF16)


def first_kernel(own_ref, r1, r2, r3, slope_ref, xo_ref, xr_ref, dw2_ref, keep_ref, give_ref, acc):
    core = lax.rem(lax.axis_index("space"), 2)
    back = (own_ref[...] + r1[...].astype(F32)) + (r2[...].astype(F32) + r3[...].astype(F32))
    gf = (back * slope_ref[...]).astype(BF16)
    left = height_taps(lambda d, h: gf[:, (d * 4 + h) * W : (d * 4 + h + 1) * W])
    col = jnp.concatenate(
        [
            jnp.concatenate(
                [input_row(xo_ref, xr_ref, d + 1 + a, h + 2) for d in range(2) for h in range(6)], axis=1
            )
            for a in range(3)
        ],
        axis=0,
    )
    dw = lax.dot_general(left, col, NT, preferred_element_type=F32)
    parts = [dw[b * 32 : (b + 1) * 32] for b in range(3)]
    acc[:, :K2] = dw2_ref[...]
    acc[:, K2:] = jnp.concatenate(parts + [jnp.zeros((32, 2 * HALF - K2 - K1), F32)], axis=1)
    keep_ref[...] = acc[:, lanes(core)]
    give_ref[...] = acc[:, lanes(1 - core)]


def chip_kernel(keep_ref, got_ref, y_ref, o0, y0, s1, s2, s3, acc, yacc):
    x, _ = split()
    acc[...] = keep_ref[...] + got_ref[...]
    yacc[...] = y_ref[...].astype(F32)
    o0[...] = acc[rows8(x), :]
    y0[...] = yacc[rows8(x), :]
    for k, out in enumerate((s1, s2, s3)):
        at = rows8(xor(x, k + 1))
        out[...] = jnp.concatenate([acc[at, :], yacc[at, :]], axis=1).astype(BF16)


def sum_kernel(o0, y0, r1, r2, r3, dw_ref, y_ref):
    x, _ = split()
    parts = [r[...].astype(F32) for r in (r1, r2, r3)]
    dw_ref[...] = ((o0[...] + parts[0][:, :HALF]) + (parts[1][:, :HALF] + parts[2][:, :HALF])).astype(BF16)
    for k, v in enumerate([y0[...]] + [r[:, HALF:] for r in parts]):
        h0 = xor(x, k) * 4
        for d in range(2):
            for h in range(4):
                at = (d * 4 + h) * W
                y_ref[d, h0 + h] = v[:, at : at + W]


def last_kernel(own_ref, got_ref, dw1_ref, dw2_ref):
    core = lax.rem(lax.axis_index("space"), 2)
    own, got = own_ref[...], got_ref[...]
    both = [jnp.where(core == 0, own, got), jnp.where(core == 0, got, own)]
    both = jnp.concatenate(both, axis=1) * (1.0 / 256.0)
    for t in range(27):
        a, b, c = t // 9, t // 3 % 3, t % 3
        at = K2 + b * 576 + a * 192 + c * 64
        dw2_ref[t] = both[:, t * W : (t + 1) * W]
        dw1_ref[t] = both[:, at : at + 64]


def local(act_in, w_first, w_second, grad_out):
    X = [[(z * 4 + x, z * 4 + (x ^ k)) for z in range(4) for x in range(4)] for k in range(4)]
    Z = [[(z * 4 + x, (z ^ k) * 4 + x) for z in range(4) for x in range(4)] for k in range(4)]
    across = [(i, (i + 1) % 8 if i % 2 else (i + 7) % 8) for i in range(8)]
    other = [(i, i ^ 1) for i in range(8)]
    x = lax.rem(lax.axis_index("filt"), 4)

    (w0,) = run(pack_first_kernel, [sds((8, K1P), BF16)], [jnp.transpose(w_first, (0, 2, 1))])
    joint = ("space", "filt")

    def zed(k0, k1):
        return [(p * 16 + f, p * 16 + (f ^ (4 * (k1 if p % 2 else k0)))) for p in range(8) for f in range(16)]

    p1 = lax.ppermute(w0, joint, zed(1, 2))
    p2 = lax.ppermute(w0, joint, zed(0, 3))

    act_in, w_second, grad_out, w0 = lax.optimization_barrier((act_in, w_second, grad_out, w0))
    rows = jnp.pad(jnp.transpose(act_in[0], (1, 2, 0, 3)), ((0, 0), (3, 3), (0, 0), (0, 0)))
    xo = lax.dynamic_slice_in_dim(rows, x * 4, 10, axis=1).reshape(20, 64, W)
    a = run(
        prepare_kernel,
        [sds((8, K1P + 12 * W), BF16)] * 4,
        [jnp.transpose(w_second, (0, 2, 1)), grad_out[0]],
        [pltpu.VMEM((2, 18, 8, W), F32), pltpu.VMEM((8, K2), F32)],
        10**9,
    )
    xo, p1 = lax.optimization_barrier((xo, p1))
    xchip = lax.ppermute(xo, "space", other)
    xnext = lax.ppermute(xo, "space", across)

    a, p1, p2 = lax.optimization_barrier((a, p1, p2))
    b = run(pack_kernel, [sds((8, 3 * K1P + 12 * W), BF16)] * 4, [w0, p1, p2] + list(a))
    b = [b[0]] + [lax.ppermute(b[k], "filt", X[k]) for k in (1, 2, 3)]
    half, go = run(
        order_kernel,
        [sds((96, K1P), BF16), sds((32, 12 * W), BF16)],
        b,
        [pltpu.VMEM((96, K1P), F32), pltpu.VMEM((32, 12 * W), F32)],
    )
    half_got = lax.ppermute(half, "space", other)

    (xw,) = run(widen_own_kernel, [sds((20, 192, W), BF16)], [xo], flops=3 * 10**8)
    (xr,) = run(widen_rim_kernel, [sds((40, 192, W), BF16)], [xchip, xnext], flops=6 * 10**8)
    slope, xa = run(
        conv_first_kernel,
        [sds((32, 1024), F32), sds((32, 384, W), BF16)],
        [half, half_got, xw, xr],
        [pltpu.VMEM((32, 128, W), F32)],
        4 * 10**9,
    )
    y, gs0, gs1, gchip, gnext, w2b = run(
        conv_second_kernel,
        [sds((32, 1024), BF16)] + [sds((6, 32, W), BF16)] * 4 + [sds((128, KB), BF16)],
        [half, half_got, go, xa],
        [pltpu.VMEM((32, K2), F32), pltpu.VMEM((32, K2), BF16)],
    )
    gchip = lax.ppermute(gchip, "space", other)
    gnext = lax.ppermute(gnext, "space", across)
    (dw2,) = run(second_kernel, [sds((32, K2), F32)], [xa, gs0, gs1], flops=25 * 10**8)

    own, *s = run(
        back_kernel,
        [sds((32, 1024), F32)] + [sds((32, 1024), BF16)] * 3,
        [gs0, gs1, gchip, gnext, w2b],
        [pltpu.VMEM((24, 96, W), BF16), pltpu.VMEM((128, 1024), F32)],
    )
    s, dw2 = lax.optimization_barrier((s, dw2))
    s = [lax.ppermute(s[k - 1], "filt", Z[k]) for k in (1, 2, 3)]

    keep, give = run(
        first_kernel,
        [sds((32, HALF), F32)] * 2,
        [own] + s + [slope, xw, xr, dw2],
        [pltpu.VMEM((32, 2 * HALF), F32)],
    )
    got = lax.ppermute(give, "space", other)
    o, yo, *s = run(
        chip_kernel,
        [sds((8, HALF), F32), sds((8, 1024), F32)] + [sds((8, HALF + 1024), BF16)] * 3,
        [keep, got, y],
        [pltpu.VMEM((32, HALF), F32), pltpu.VMEM((32, 1024), F32)],
    )
    s = [lax.ppermute(s[k - 1], "filt", X[k]) for k in (1, 2, 3)]
    part, yt = run(sum_kernel, [sds((8, HALF), BF16), sds((2, 16, 8, W), F32)], [o, yo] + s)
    y_out = jnp.transpose(yt, (2, 0, 1, 3)).astype(BF16)[None]

    q = [part] + [lax.ppermute(part, "space", [(i, i ^ (2 * k)) for i in range(8)]) for k in (1, 2, 3)]
    q = [v.astype(F32) for v in q]
    part = ((q[0] + q[1]) + (q[2] + q[3])).astype(BF16)
    part = part.astype(F32) + lax.ppermute(part, "sample", [(0, 1), (1, 0)]).astype(F32)
    got = lax.ppermute(part, "space", other)
    dw1, dw2 = run(last_kernel, [sds((27, 8, 64), F32), sds((27, 8, 128), F32)], [part, got])
    return y_out, jnp.transpose(dw1, (0, 2, 1)), jnp.transpose(dw2, (0, 2, 1))


def solution(mesh):
    placed = (
        P("sample", None, "space", None, None),
        P(None, None, "filt"),
        P(None, None, "filt"),
        P("sample", "filt", "space", None, None),
    )
    return jax.shard_map(
        local,
        mesh=mesh,
        in_specs=placed,
        out_specs=(
            P("sample", "filt", "space", None, None),
            P(None, None, "filt"),
            P(None, None, "filt"),
        ),
        check_vma=False,
    )
```

```python
import jax
import jax.numpy as jnp
from jax import lax
from jax.experimental import pallas as pl
from jax.experimental.pallas import tpu as pltpu
from jax.sharding import PartitionSpec as P

F32 = jnp.float32
BF16 = jnp.bfloat16
W = 128
K1, K2 = 27 * 64, 27 * 128
K1P = 1792
HALF = 2688
KB = 896
VMEM = pl.BlockSpec(memory_space=pltpu.VMEM)
NT = (((1,), (1,)), ((), ()))


def run(kernel, outs, args, scratch=(), flops=10**8):
    return pl.pallas_call(
        kernel,
        out_shape=outs,
        in_specs=[VMEM] * len(args),
        out_specs=[VMEM] * len(outs),
        scratch_shapes=list(scratch),
        cost_estimate=pl.CostEstimate(flops=flops, bytes_accessed=10**5, transcendentals=0),
        compiler_params=pltpu.CompilerParams(vmem_limit_bytes=20 * 1024 * 1024),
    )(*args)


def sds(shape, dtype):
    return jax.ShapeDtypeStruct(shape, dtype)


def split():
    f = lax.axis_index("filt")
    return lax.rem(f, 4), lax.div(f, 4)


def xor(a, k):
    return lax.bitwise_xor(a, jnp.int32(k))


def rows8(i):
    return pl.ds(pl.multiple_of(i * 8, 8), 8)


def rows32(i):
    return pl.ds(pl.multiple_of(i * 32, 32), 32)


def lanes(core):
    return pl.ds(pl.multiple_of(core * HALF, W), HALF)


def shifted(x):
    lane = lax.broadcasted_iota(jnp.int32, x.shape, 1)
    left = jnp.where(lane == 0, 0.0, pltpu.roll(x, 1, 1))
    right = jnp.where(lane == W - 1, 0.0, pltpu.roll(x, W - 1, 1))
    return left, x, right


def height_taps(row):
    zero = jnp.zeros((32, W), BF16)
    taps = []
    for b in range(3):
        cells = []
        for d in range(2):
            cells += [zero] * b + [row(d, h) for h in range(4)] + [zero] * (2 - b)
        taps.append(jnp.concatenate(cells, axis=1))
    return jnp.concatenate(taps, axis=0)


def logistic(v):
    return 0.5 * jnp.tanh(0.5 * v) + 0.5


def pack_first_kernel(w1_ref, out):
    w1 = [w1_ref[t].astype(F32) for t in range(27)]
    out[...] = jnp.concatenate(w1 + [jnp.zeros((8, K1P - K1), F32)], axis=1).astype(BF16)


def prepare_kernel(w2_ref, g_ref, b0, b1, b2, b3, rows_ref, acc):
    x, _ = split()
    core = lax.rem(lax.axis_index("space"), 2)
    for t in range(27):
        acc[:, t * W : (t + 1) * W] = w2_ref[t].astype(F32)
    w2 = acc[:, pl.ds(pl.multiple_of(core * (13 * W), W), K1P)]
    for d in range(2):
        t = jnp.swapaxes(g_ref[:, d].astype(F32), 0, 1)
        rows_ref[d, 0] = jnp.zeros((8, W), F32)
        rows_ref[d, 17] = jnp.zeros((8, W), F32)
        rows_ref[d, 1:17] = t
    for k, out in enumerate((b0, b1, b2, b3)):
        h0 = xor(x, k) * 4
        parts = [rows_ref[d, h0 + h] for d in range(2) for h in range(6)]
        out[...] = jnp.concatenate([w2] + parts, axis=1).astype(BF16)


def pack_kernel(w0_ref, p1_ref, p2_ref, a0, a1, a2, a3, b0, b1, b2, b3):
    _, zl = split()
    core = lax.rem(lax.axis_index("space"), 2)
    w0, p1, p2 = w0_ref[...], p1_ref[...], p2_ref[...]
    same, other = jnp.where(core == 0, w0, p1), jnp.where(core == 0, p1, p2)
    even = lax.rem(zl, 2) == 0
    low, high = jnp.where(even, same, other), jnp.where(even, other, same)
    for a, b in zip((a0, a1, a2, a3), (b0, b1, b2, b3)):
        b[:, :K1P] = low
        b[:, K1P : 2 * K1P] = high
        b[:, 2 * K1P :] = a[...]


def order_kernel(b0, b1, b2, b3, half_ref, go_ref, acc, acc_go):
    x, _ = split()
    for k, b in enumerate((b0, b1, b2, b3)):
        v = b[...].astype(F32)
        for j in range(3):
            acc[rows8(j * 4 + xor(x, k)), :] = v[:, j * K1P : (j + 1) * K1P]
        acc_go[rows8(xor(x, k)), :] = v[:, 3 * K1P :]
    half_ref[...] = acc[...].astype(BF16)
    go_ref[...] = acc_go[...].astype(BF16)


def widen(v, out, r):
    for k, part in enumerate(shifted(v)):
        out[r, k * 64 : (k + 1) * 64] = part.astype(BF16)


def widen_own_kernel(xo_ref, own_ref):
    for r in range(20):
        widen(xo_ref[r].astype(F32), own_ref, r)


def widen_rim_kernel(chip_ref, next_ref, rim_ref):
    p = lax.axis_index("space")
    first = lax.rem(p, 2) == 0
    for r in range(20):
        chip, far = chip_ref[r].astype(F32), next_ref[r].astype(F32)
        widen(jnp.where(p > 0, jnp.where(first, far, chip), 0.0), rim_ref, r)
        widen(jnp.where(p < 7, jnp.where(first, chip, far), 0.0), rim_ref, 20 + r)


def input_row(own_ref, rim_ref, layer, height):
    if 2 <= layer <= 3:
        return own_ref[(layer - 2) * 10 + height]
    return rim_ref[(layer if layer < 2 else layer - 2) * 10 + height]


def conv_first_kernel(own_ref, got_ref, xo_ref, xr_ref, slope_ref, xa_ref, zs):
    x, zl = split()
    p = lax.axis_index("space")
    own, got = own_ref[:64], got_ref[:64]
    first = lax.rem(lax.div(zl, 2) + p, 2) == 0
    w1 = jnp.concatenate([jnp.where(first, own, got), jnp.where(first, got, own)], axis=0)[:, :K1]

    for i in range(16):
        dd, hh = i // 4, i % 4 * 2
        cols = []
        for j in range(2):
            cols.append(
                jnp.concatenate(
                    [input_row(xo_ref, xr_ref, dd + a, hh + j + b) for a in range(3) for b in range(3)], axis=0
                )
            )
        z = jnp.dot(w1, jnp.concatenate(cols, axis=1), preferred_element_type=F32)
        depth = p * 2 - 1 + dd
        for j in range(2):
            height = x * 4 - 2 + hh + j
            inside = (depth >= 0) & (depth < 16) & (height >= 0) & (height < 16)
            zr = z[:, j * W : (j + 1) * W]
            r = dd * 8 + hh + j
            zs[r] = zr
            act = jnp.where(inside, zr * logistic(zr), 0.0).astype(BF16).astype(F32)
            left, mid, right = shifted(act)
            xa_ref[r, 0:128] = left.astype(BF16)
            xa_ref[r, 128:256] = mid.astype(BF16)
            xa_ref[r, 256:384] = right.astype(BF16)

    for d in range(2):
        for h in range(4):
            v = zs[(d + 1) * 8 + h + 2, rows32(zl), :]
            q = logistic(v)
            slope_ref[:, (d * 4 + h) * W : (d * 4 + h + 1) * W] = q * (1.0 + v * (1.0 - q))


def conv_second_kernel(
    own_ref, got_ref, go_ref, xa_ref, y_ref, gs0_ref, gs1_ref, chip_ref, next_ref, w2b_ref, acc, w2_ref
):
    first = lax.rem(lax.axis_index("space"), 2) == 0
    own, got = own_ref[64:], got_ref[64:]
    w2_ref[:, : 14 * W] = jnp.where(first, own, got)
    w2_ref[:, 14 * W :] = jnp.where(first, got, own)[:, W:]
    acc[...] = w2_ref[...].astype(F32)
    for j in range(7):
        taps = [acc[:, t * W : (t + 1) * W] if t < 27 else jnp.zeros((32, W), F32) for t in range(4 * j, 4 * j + 4)]
        w2b_ref[:, j * W : (j + 1) * W] = jnp.concatenate(taps, axis=0).T.astype(BF16)
    planes = [[], []]
    for dd in range(4):
        taps = [a for a in range(3) if 0 <= dd - a <= 1]
        w = jnp.concatenate(
            [w2_ref[:, t * 384 : (t + 1) * 384] for a in taps for t in range(3 * a, 3 * a + 3)], axis=0
        )
        col = jnp.concatenate([xa_ref[dd * 8 + h] for h in range(8)], axis=1)
        part = jnp.dot(w, col, preferred_element_type=F32)
        for k, a in enumerate(taps):
            for b in range(3):
                at = (k * 3 + b) * 32
                planes[dd - a].append(part[at : at + 32, b * W : (b + 6) * W])
    for d in range(2):
        t = planes[d]
        z = ((t[0] + t[1]) + (t[2] + t[3])) + ((t[4] + t[5]) + (t[6] + t[7])) + t[8]
        for hh in range(6):
            v = z[:, hh * W : (hh + 1) * W]
            q = logistic(v)
            if 1 <= hh <= 4:
                at = (d * 4 + hh - 1) * W
                y_ref[:, at : at + W] = (v * q).astype(BF16)
            g = go_ref[:, (d * 6 + hh) * W : (d * 6 + hh + 1) * W].astype(F32)
            gs = (g * (q * (1.0 + v * (1.0 - q)))).astype(BF16)
            (gs0_ref if d == 0 else gs1_ref)[hh] = gs
    for hh in range(6):
        chip_ref[hh] = jnp.where(first, gs1_ref[hh], gs0_ref[hh])
        next_ref[hh] = jnp.where(first, gs0_ref[hh], gs1_ref[hh])


def second_kernel(xa_ref, gs0_ref, gs1_ref, dw_ref):
    left = height_taps(lambda d, h: (gs0_ref, gs1_ref)[d][h + 1])
    for a in range(3):
        col = jnp.concatenate([xa_ref[(d + a) * 8 + h + 1] for d in range(2) for h in range(6)], axis=1)
        dw = lax.dot_general(left, col, NT, preferred_element_type=F32)
        for b in range(3):
            at = (a * 3 + b) * 384
            dw_ref[:, at : at + 384] = dw[b * 32 : (b + 1) * 32]


def back_kernel(gs0_ref, gs1_ref, chip_ref, next_ref, w2b_ref, own_ref, s1, s2, s3, g3, acc):
    _, zl = split()
    p = lax.axis_index("space")
    first = lax.rem(p, 2) == 0
    for d in range(4):
        for h in range(6):
            if d == 0:
                v = jnp.where(first, next_ref[h].astype(F32), chip_ref[h].astype(F32))
                v = jnp.where(p > 0, v, 0.0)
            elif d == 3:
                v = jnp.where(first, chip_ref[h].astype(F32), next_ref[h].astype(F32))
                v = jnp.where(p < 7, v, 0.0)
            else:
                v = (gs0_ref, gs1_ref)[d - 1][h].astype(F32)
            before, mid, after = shifted(v)
            g3[d * 6 + h, 0:32] = after.astype(BF16)
            g3[d * 6 + h, 32:64] = mid.astype(BF16)
            g3[d * 6 + h, 64:96] = before.astype(BF16)
    w = w2b_ref[...]
    for d in range(2):
        for hp in range(2):
            cols = []
            for j in range(2):
                h = hp * 2 + j
                cols.append(
                    jnp.concatenate(
                        [g3[(d + 2 - a) * 6 + h + 2 - b] for a in range(3) for b in range(3)]
                        + [jnp.zeros((32, W), BF16)],
                        axis=0,
                    )
                )
            at = (d * 4 + hp * 2) * W
            acc[:, at : at + 2 * W] = jnp.dot(w, jnp.concatenate(cols, axis=1), preferred_element_type=F32)
    own_ref[...] = acc[rows32(zl), :]
    for k, out in enumerate((s1, s2, s3)):
        out[...] = acc[rows32(xor(zl, k + 1)), :].astype(BF16)


def first_kernel(own_ref, r1, r2, r3, slope_ref, xo_ref, xr_ref, dw2_ref, keep_ref, give_ref, acc):
    core = lax.rem(lax.axis_index("space"), 2)
    back = (own_ref[...] + r1[...].astype(F32)) + (r2[...].astype(F32) + r3[...].astype(F32))
    gf = (back * slope_ref[...]).astype(BF16)
    left = height_taps(lambda d, h: gf[:, (d * 4 + h) * W : (d * 4 + h + 1) * W])
    col = jnp.concatenate(
        [
            jnp.concatenate(
                [input_row(xo_ref, xr_ref, d + 1 + a, h + 2) for d in range(2) for h in range(6)], axis=1
            )
            for a in range(3)
        ],
        axis=0,
    )
    dw = lax.dot_general(left, col, NT, preferred_element_type=F32)
    parts = [dw[b * 32 : (b + 1) * 32] for b in range(3)]
    acc[:, :K2] = dw2_ref[...]
    acc[:, K2:] = jnp.concatenate(parts + [jnp.zeros((32, 2 * HALF - K2 - K1), F32)], axis=1)
    keep_ref[...] = acc[:, lanes(core)]
    give_ref[...] = acc[:, lanes(1 - core)]


def chip_kernel(keep_ref, got_ref, y_ref, o0, y0, s1, s2, s3, acc, yacc):
    x, _ = split()
    acc[...] = keep_ref[...] + got_ref[...]
    yacc[...] = y_ref[...].astype(F32)
    o0[...] = acc[rows8(x), :]
    y0[...] = yacc[rows8(x), :]
    for k, out in enumerate((s1, s2, s3)):
        at = rows8(xor(x, k + 1))
        out[...] = jnp.concatenate([acc[at, :], yacc[at, :]], axis=1).astype(BF16)


def sum_kernel(o0, y0, r1, r2, r3, dw_ref, y_ref):
    x, _ = split()
    parts = [r[...].astype(F32) for r in (r1, r2, r3)]
    dw_ref[...] = ((o0[...] + parts[0][:, :HALF]) + (parts[1][:, :HALF] + parts[2][:, :HALF])).astype(BF16)
    for k, v in enumerate([y0[...]] + [r[:, HALF:] for r in parts]):
        h0 = xor(x, k) * 4
        for d in range(2):
            for h in range(4):
                at = (d * 4 + h) * W
                y_ref[d, h0 + h] = v[:, at : at + W]


def last_kernel(own_ref, got_ref, dw1_ref, dw2_ref):
    core = lax.rem(lax.axis_index("space"), 2)
    own, got = own_ref[...], got_ref[...]
    both = [jnp.where(core == 0, own, got), jnp.where(core == 0, got, own)]
    both = jnp.concatenate(both, axis=1) * (1.0 / 256.0)
    for t in range(27):
        a, b, c = t // 9, t // 3 % 3, t % 3
        at = K2 + b * 576 + a * 192 + c * 64
        dw2_ref[t] = both[:, t * W : (t + 1) * W]
        dw1_ref[t] = both[:, at : at + 64]


def local(act_in, w_first, w_second, grad_out):
    X = [[(z * 4 + x, z * 4 + (x ^ k)) for z in range(4) for x in range(4)] for k in range(4)]
    Z = [[(z * 4 + x, (z ^ k) * 4 + x) for z in range(4) for x in range(4)] for k in range(4)]
    across = [(i, (i + 1) % 8 if i % 2 else (i + 7) % 8) for i in range(8)]
    other = [(i, i ^ 1) for i in range(8)]
    x = lax.rem(lax.axis_index("filt"), 4)

    (w0,) = run(pack_first_kernel, [sds((8, K1P), BF16)], [jnp.transpose(w_first, (0, 2, 1))])
    joint = ("space", "filt")

    def zed(k0, k1):
        return [(p * 16 + f, p * 16 + (f ^ (4 * (k1 if p % 2 else k0)))) for p in range(8) for f in range(16)]

    p1 = lax.ppermute(w0, joint, zed(1, 2))
    p2 = lax.ppermute(w0, joint, zed(0, 3))

    act_in, w_second, grad_out, w0 = lax.optimization_barrier((act_in, w_second, grad_out, w0))
    rows = jnp.pad(jnp.transpose(act_in[0], (1, 2, 0, 3)), ((0, 0), (3, 3), (0, 0), (0, 0)))
    xo = lax.dynamic_slice_in_dim(rows, x * 4, 10, axis=1).reshape(20, 64, W)
    a = run(
        prepare_kernel,
        [sds((8, K1P + 12 * W), BF16)] * 4,
        [jnp.transpose(w_second, (0, 2, 1)), grad_out[0]],
        [pltpu.VMEM((2, 18, 8, W), F32), pltpu.VMEM((8, K2), F32)],
        10**9,
    )
    xo, p1 = lax.optimization_barrier((xo, p1))
    xchip = lax.ppermute(xo, "space", other)
    xnext = lax.ppermute(xo, "space", across)

    a, p1, p2 = lax.optimization_barrier((a, p1, p2))
    b = run(pack_kernel, [sds((8, 3 * K1P + 12 * W), BF16)] * 4, [w0, p1, p2] + list(a))
    far = {k: lax.ppermute(b[k], "filt", X[k]) for k in (2, 3, 1)}
    b = [b[0], far[1], far[2], far[3]]
    half, go = run(
        order_kernel,
        [sds((96, K1P), BF16), sds((32, 12 * W), BF16)],
        b,
        [pltpu.VMEM((96, K1P), F32), pltpu.VMEM((32, 12 * W), F32)],
    )
    half_got = lax.ppermute(half, "space", other)

    (xw,) = run(widen_own_kernel, [sds((20, 192, W), BF16)], [xo], flops=3 * 10**8)
    (xr,) = run(widen_rim_kernel, [sds((40, 192, W), BF16)], [xchip, xnext], flops=6 * 10**8)
    slope, xa = run(
        conv_first_kernel,
        [sds((32, 1024), F32), sds((32, 384, W), BF16)],
        [half, half_got, xw, xr],
        [pltpu.VMEM((32, 128, W), F32)],
        4 * 10**9,
    )
    y, gs0, gs1, gchip, gnext, w2b = run(
        conv_second_kernel,
        [sds((32, 1024), BF16)] + [sds((6, 32, W), BF16)] * 4 + [sds((128, KB), BF16)],
        [half, half_got, go, xa],
        [pltpu.VMEM((32, K2), F32), pltpu.VMEM((32, K2), BF16)],
    )
    gchip = lax.ppermute(gchip, "space", other)
    gnext = lax.ppermute(gnext, "space", across)
    (dw2,) = run(second_kernel, [sds((32, K2), F32)], [xa, gs0, gs1], flops=25 * 10**8)

    own, *s = run(
        back_kernel,
        [sds((32, 1024), F32)] + [sds((32, 1024), BF16)] * 3,
        [gs0, gs1, gchip, gnext, w2b],
        [pltpu.VMEM((24, 96, W), BF16), pltpu.VMEM((128, 1024), F32)],
    )
    s, dw2 = lax.optimization_barrier((s, dw2))
    s = [lax.ppermute(s[k - 1], "filt", Z[k]) for k in (1, 2, 3)]

    keep, give = run(
        first_kernel,
        [sds((32, HALF), F32)] * 2,
        [own] + s + [slope, xw, xr, dw2],
        [pltpu.VMEM((32, 2 * HALF), F32)],
    )
    got = lax.ppermute(give, "space", other)
    o, yo, *s = run(
        chip_kernel,
        [sds((8, HALF), F32), sds((8, 1024), F32)] + [sds((8, HALF + 1024), BF16)] * 3,
        [keep, got, y],
        [pltpu.VMEM((32, HALF), F32), pltpu.VMEM((32, 1024), F32)],
    )
    s = [lax.ppermute(s[k - 1], "filt", X[k]) for k in (1, 2, 3)]
    part, yt = run(sum_kernel, [sds((8, HALF), BF16), sds((2, 16, 8, W), F32)], [o, yo] + s)
    y_out = jnp.transpose(yt, (2, 0, 1, 3)).astype(BF16)[None]

    q = [part] + [lax.ppermute(part, "space", [(i, i ^ (2 * k)) for i in range(8)]) for k in (1, 2, 3)]
    q = [v.astype(F32) for v in q]
    part = ((q[0] + q[1]) + (q[2] + q[3])).astype(BF16)
    part = part.astype(F32) + lax.ppermute(part, "sample", [(0, 1), (1, 0)]).astype(F32)
    got = lax.ppermute(part, "space", other)
    dw1, dw2 = run(last_kernel, [sds((27, 8, 64), F32), sds((27, 8, 128), F32)], [part, got])
    return y_out, jnp.transpose(dw1, (0, 2, 1)), jnp.transpose(dw2, (0, 2, 1))


def solution(mesh):
    placed = (
        P("sample", None, "space", None, None),
        P(None, None, "filt"),
        P(None, None, "filt"),
        P("sample", "filt", "space", None, None),
    )
    return jax.shard_map(
        local,
        mesh=mesh,
        in_specs=placed,
        out_specs=(
            P("sample", "filt", "space", None, None),
            P(None, None, "filt"),
            P(None, None, "filt"),
        ),
        check_vma=False,
    )
```
